512 devices in a mesh: aa: 8 (over z_hi, y), ba: 8 (over z_lo), col: 8 (over x, core).
Axes of the slice: x: 4, y: 4, z: 16 (z_hi: 2, z_lo: 8; z = z_hi * 8 + z_lo), core: 2. Of those that a mesh axis runs over, the one named last changes fastest.
Arguments:
- amplitudes: bfloat16 [384, 384, 384], P('aa', 'ba', 'col'), as said below
- factors: bfloat16 [4, 384, 384], replicated, may hold values from -0.15625 to 0.15625
- energies: float32 [384], replicated, may hold values from 0.3 to 1.5
Outputs:
- sigma: bfloat16 [384, 384, 384], P('aa', 'ba', 'col')
The draws below stay inside these ranges and needn't reach their ends.
Inputs may be any that keep to these rules, and one draw needn't show every extreme that they name: amplitudes is antisymmetric: exchanging any two of its three indices changes its sign.
All inputs are finite; a program needn't handle non-finite values.
Results may differ from the reference program's by a relative error of at most 0.0065.
Values may be sent and summed in bfloat16 or wider, within the bound.
No kernel may reach another device: no remote copies, remote signals or barrier semaphores. Data moves between devices by JAX's collectives and lax.ppermute only.
A program may use at most 128 MiB of HBM per device.

```python
import jax
import jax.numpy as jnp
from jax import lax

V = 384
NAUX = 4


def draw_amplitudes(key, part):
    source = jax.random.normal(key, (V, V, V), jnp.float32)
    even = source + jnp.transpose(source, (1, 2, 0)) + jnp.transpose(source, (2, 0, 1))
    odd_part = jnp.transpose(source, (1, 0, 2)) + jnp.transpose(source, (0, 2, 1)) + jnp.transpose(source, (2, 1, 0))
    return ((even - odd_part) / 2.449489742783178).astype(jnp.bfloat16)


def centred(key, dims, deviation, most, held_as=jnp.bfloat16):
    array = jax.random.normal(key, dims, jnp.float32) * deviation
    return jnp.minimum(jnp.maximum(array, -most), most).astype(held_as)


def setup_inputs(seed: int = 0) -> dict:
    key_list = jax.random.split(jax.random.key(seed), 4)
    return {
        "amplitudes": draw_amplitudes(jax.random.fold_in(key_list[3], 71), 0),
        "factors": centred(key_list[1], (NAUX, V, V), (4 * V) ** -0.5, 0.15625),
        "energies": jnp.clip(jax.random.uniform(key_list[2], (V,), jnp.float32, 0.3, 1.5), 0.3, 1.5),
    }


def reference(amplitudes, factors, energies):
    amps = amplitudes.astype(jnp.float32)

    def step(running, matrix):
        factor = matrix.astype(jnp.float32)
        along_a = jnp.einsum("ae,ebc->abc", factor, amps)
        along_b = jnp.einsum("be,aec->abc", factor, amps)
        along_a = lax.optimization_barrier(along_a.astype(jnp.bfloat16)).astype(jnp.float32)
        along_b = lax.optimization_barrier(along_b.astype(jnp.bfloat16)).astype(jnp.float32)
        ladder_ab = jnp.einsum("afc,bf->abc", along_a, factor)
        ladder_ac = jnp.einsum("abf,cf->abc", along_a, factor)
        ladder_bc = jnp.einsum("abf,cf->abc", along_b, factor)
        return running + ladder_ab + ladder_bc + ladder_ac, None

    start_sum = jnp.zeros((V, V, V), jnp.float32)
    total_sum, unused = lax.scan(step, start_sum, factors)
    shifts = energies[:, None, None] + energies[None, :, None] + energies[None, None, :]
    return (2.0 * total_sum + shifts * amps).astype(jnp.bfloat16)
```

```python
import jax
import jax.numpy as jnp
from jax import lax
from jax.sharding import Mesh, PartitionSpec as P

ALL = ("zh", "y", "zl", "x", "core")
PLANE = ("y", "x", "core")


def moved(array, place):
    pairs = []
    for i in range(8):
        for j in range(8):
            for k in range(8):
                a, b, c = place(i, j, k)
                pairs.append(((a * 8 + b) * 8 + c, (i * 8 + j) * 8 + k))
    return lax.ppermute(array, ALL, pairs)


def on_device(amplitudes, factors, energies):
    w = amplitudes.shape[0]
    half = lax.axis_index("zh")
    index_a = half * 4 + lax.axis_index("y")
    index_b = lax.axis_index("zl")
    index_c = lax.axis_index("x") * 2 + lax.axis_index("core")
    energy_a = lax.dynamic_slice_in_dim(energies, index_a * w, w, 0)
    energy_b = lax.dynamic_slice_in_dim(energies, index_b * w, w, 0)
    energy_c = lax.dynamic_slice_in_dim(energies, index_c * w, w, 0)

    parts = amplitudes.reshape(w, 24, 2, w).transpose(1, 0, 2, 3).reshape(24, w, 2 * w)
    parts = jnp.pad(parts, ((0, 8), (0, 0), (0, 0)))
    parts = lax.all_to_all(parts, PLANE, split_axis=0, concat_axis=0, tiled=True)
    rows = parts.reshape(4, 8, w, 2, w).transpose(3, 0, 2, 1, 4).reshape(2, 4 * w, 8 * w)
    near = lax.dynamic_slice_in_dim(rows, half * 4 * w, 4 * w, 2)
    across = lax.dynamic_slice_in_dim(rows, (1 - half) * 4 * w, 4 * w, 2)
    far = lax.ppermute(near, "zh", [(0, 1), (1, 0)])
    whole = jnp.concatenate(
        [jnp.concatenate([near, across], 2), jnp.concatenate([-across.transpose(0, 2, 1), far], 2)], 1
    )
    turned = jnp.where(half == 0, factors, jnp.roll(factors, 4 * w, 2))
    mine = lax.dynamic_slice_in_dim(turned, half * 4 * w, 4 * w, 1)
    along = jnp.einsum("pae,bef->bpaf", mine, whole, preferred_element_type=jnp.float32).astype(jnp.bfloat16)
    close = jnp.einsum("bpaf,pcf->bac", along, turned, preferred_element_type=jnp.float32).astype(jnp.bfloat16)
    close = close.reshape(2, 4, w, 8, w).transpose(1, 3, 2, 0, 4).reshape(32, w, 2 * w)
    close = lax.all_to_all(close, PLANE, split_axis=0, concat_axis=0, tiled=True)
    own = close[:24].reshape(24, w, 2, w).transpose(1, 0, 2, 3).reshape(w, w, w)
    flat = own.reshape(w, w * w)
    swap_ab = moved(flat, lambda i, j, k: (j, i, k)).reshape(w, w, w).transpose(1, 0, 2)
    swap_bc = moved(flat, lambda i, j, k: (i, k, j)).reshape(w, w, w).transpose(0, 2, 1)
    ladders = own.astype(jnp.float32) - swap_ab.astype(jnp.float32) - swap_bc.astype(jnp.float32)
    shifts = energy_a[:, None, None] + energy_b[None, :, None] + energy_c[None, None, :]
    result = 2.0 * ladders + shifts * amplitudes.astype(jnp.float32)
    return result.astype(jnp.bfloat16)


def solution(mesh):
    fine = Mesh(mesh.devices.reshape(2, 4, 8, 4, 2), ALL)
    place = P(("zh", "y"), "zl", ("x", "core"))
    return jax.shard_map(on_device, mesh=fine, in_specs=(place, P(), P()), out_specs=place, check_vma=False)
```

```python
import functools

import jax
import jax.numpy as jnp
import numpy as np
from jax import lax
from jax.experimental import pallas as pl
from jax.experimental.pallas import tpu as pltpu
from jax.sharding import Mesh, PartitionSpec as P

ALL = ("zh", "y", "zl", "x", "core")
PLANE = ("y", "x", "core")
UPPER = [(u, v) for u in range(4) for v in range(u, 4)]
MASKS = (389, 85, 114, 41, 49)


def slot(i, j, k):
    bits = k | (i & 3) << 3 | j << 5 | (i >> 2) << 8
    core, x_low, x_high, y_low, y_high = (bin(bits & mask).count("1") & 1 for mask in MASKS)
    return (y_high * 2 + y_low) * 8 + x_high * 4 + x_low * 2 + core


def holder(i, j, k):
    place = slot(i, j, k)
    return (((i >> 2) * 4 + place // 8) * 8 + j) * 8 + place % 8


def moved(array, target):
    pairs = []
    for i in range(8):
        for j in range(8):
            for k in range(8):
                a, b, c = target(i, j, k)
                pairs.append((holder(i, j, k), (a * 8 + b) * 8 + c))
    return lax.ppermute(array, ALL, pairs)


def sandwich(half_ref, slot_ref, rows_ref, far_ref, factors_ref, out_ref, matrix):
    w = rows_ref.shape[1]
    half = half_ref[0]
    first = half == 0
    own = pl.ds(pl.multiple_of(half * 4 * w, 64), 4 * w)
    other = pl.ds(pl.multiple_of((1 - half) * 4 * w, 64), 4 * w)
    mine = jnp.concatenate([factors_ref[p, own, :] for p in range(4)], axis=0)
    results = []
    for b in range(2):
        part = slice(b * w, (b + 1) * w)
        near = jnp.concatenate(
            [jnp.concatenate([rows_ref[y * 8 + k, :, part] for k in range(8)], axis=1) for y in range(4)], axis=0
        )
        across = jnp.where(first, near[:, 4 * w :], near[:, : 4 * w])
        below = -across.astype(jnp.float32).T.astype(jnp.bfloat16)
        blocks = {}
        for n, (u, v) in enumerate(UPPER):
            block = far_ref[:, (2 * n + b) * w : (2 * n + b + 1) * w]
            blocks[u, v] = block
            if u != v:
                blocks[v, u] = -block.astype(jnp.float32).T.astype(jnp.bfloat16)
        far = jnp.concatenate([jnp.concatenate([blocks[u, v] for v in range(4)], axis=1) for u in range(4)], axis=0)
        matrix[own, :] = near
        matrix[other, :] = jnp.where(
            first, jnp.concatenate([below, far], axis=1), jnp.concatenate([far, below], axis=1)
        )
        along = jnp.dot(mine, matrix[...], preferred_element_type=jnp.float32).astype(jnp.bfloat16)
        total = jnp.zeros((4 * w, 8 * w), jnp.float32)
        for p in range(4):
            total += lax.dot_general(
                along[p * 4 * w : (p + 1) * 4 * w],
                factors_ref[p],
                (((1,), (1,)), ((), ())),
                preferred_element_type=jnp.float32,
            )
        results.append(total)
    for y in range(4):
        for k in range(8):
            tile = [r[y * w : (y + 1) * w, k * w : (k + 1) * w] for r in results]
            out_ref[slot_ref[y * 8 + k]] = jnp.concatenate(tile, axis=1).astype(jnp.bfloat16)


def finish(own_ref, ab_ref, bc_ref, amps_ref, shift_a_ref, shift_bc_ref, out_ref):
    w = amps_ref.shape[0]
    shift_bc = shift_bc_ref[...]
    turned = bc_ref[...].astype(jnp.float32).T
    rest = own_ref[...].astype(jnp.float32) - ab_ref[...].astype(jnp.float32)
    for a in range(w):
        part = slice(a * w, (a + 1) * w)
        ladder = rest[:, part] - turned[part]
        shift = shift_bc + shift_a_ref[a]
        out_ref[a] = (2.0 * ladder + shift * amps_ref[a].astype(jnp.float32)).astype(jnp.bfloat16)


def on_device(amplitudes, factors, energies):
    w = amplitudes.shape[0]
    half = lax.axis_index("zh")
    index_a = half * 4 + lax.axis_index("y")
    index_b = lax.axis_index("zl")
    index_c = lax.axis_index("x") * 2 + lax.axis_index("core")
    energy_a = lax.dynamic_slice_in_dim(energies, index_a * w, w, 0)
    energy_b = lax.dynamic_slice_in_dim(energies, index_b * w, w, 0)
    energy_c = lax.dynamic_slice_in_dim(energies, index_c * w, w, 0)
    shift_bc = energy_b[:, None] + energy_c[None, :]
    places = np.array([[[slot(h * 4 + y, j, k) for y in range(4) for k in range(8)] for j in range(8)] for h in range(2)])
    places = jnp.asarray(places, jnp.int32)[half, index_b]

    parts = amplitudes.reshape(w, 24, 2, w).transpose(1, 0, 2, 3).reshape(24, w, 2 * w)
    parts = jnp.pad(parts, ((0, 8), (0, 0), (0, 0)))
    parts = lax.all_to_all(parts, PLANE, split_axis=0, concat_axis=0, tiled=True)
    near = lax.dynamic_slice_in_dim(parts.reshape(4, 8, w, 2 * w), half * 4, 4, 1)
    near = jnp.concatenate([near[u, v] for u, v in UPPER], axis=1)
    far = lax.ppermute(near, "zh", [(0, 1), (1, 0)])
    smem = pl.BlockSpec(memory_space=pltpu.SMEM)
    vmem = pl.BlockSpec(memory_space=pltpu.VMEM)
    close = pl.pallas_call(
        sandwich,
        out_shape=jax.ShapeDtypeStruct((32, w, 2 * w), jnp.bfloat16),
        in_specs=[smem, smem, vmem, vmem, vmem],
        out_specs=vmem,
        scratch_shapes=[pltpu.VMEM((8 * w, 8 * w), jnp.bfloat16)],
        compiler_params=pltpu.CompilerParams(vmem_limit_bytes=40 << 20),
        name="sandwich",
    )(half.reshape(1), places, parts, far, factors)
    close = lax.all_to_all(close, PLANE, split_axis=0, concat_axis=0, tiled=True)[:24]
    first = close.transpose(1, 0, 2).reshape(w, w * w)
    second = close.reshape(24, w, 2, w).transpose(0, 2, 1, 3).reshape(w, w * w)
    swap_ab = moved(first, lambda i, j, k: (j, i, k))
    swap_bc = moved(second, lambda i, j, k: (i, k, j))
    own = moved(second, lambda i, j, k: (i, j, k))
    return pl.pallas_call(
        finish,
        out_shape=jax.ShapeDtypeStruct(amplitudes.shape, jnp.bfloat16),
        in_specs=[vmem, vmem, vmem, vmem, smem, vmem],
        out_specs=vmem,
        compiler_params=pltpu.CompilerParams(vmem_limit_bytes=40 << 20),
        name="finish",
    )(own, swap_ab, swap_bc, amplitudes, energy_a, shift_bc)


def solution(mesh):
    fine = Mesh(mesh.devices.reshape(2, 4, 8, 4, 2), ALL)
    place = P(("zh", "y"), "zl", ("x", "core"))
    return jax.shard_map(on_device, mesh=fine, in_specs=(place, P(), P()), out_specs=place, check_vma=False)
```

```python
import functools

import jax
import jax.numpy as jnp
import numpy as np
from jax import lax
from jax.experimental import pallas as pl
from jax.experimental.pallas import tpu as pltpu
from jax.sharding import Mesh, PartitionSpec as P

ALL = ("zh", "y", "zl", "x", "core")
PLANE = ("y", "x", "core")
UPPER = [(u, v) for u in range(4) for v in range(u, 4)]
LAST = (((1,), (1,)), ((), ()))
MASKS = (389, 85, 114, 41, 49)


def slot(i, j, k):
    bits = k | (i & 3) << 3 | j << 5 | (i >> 2) << 8
    core, x_low, x_high, y_low, y_high = (bin(bits & mask).count("1") & 1 for mask in MASKS)
    return (y_high * 2 + y_low) * 8 + x_high * 4 + x_low * 2 + core


def holder(i, j, k):
    place = slot(i, j, k)
    return (((i >> 2) * 4 + place // 8) * 8 + j) * 8 + place % 8


def moved(array, target):
    pairs = []
    for i in range(8):
        for j in range(8):
            for k in range(8):
                a, b, c = target(i, j, k)
                pairs.append((holder(i, j, k), (a * 8 + b) * 8 + c))
    return lax.ppermute(array, ALL, pairs)


def pack(amps_ref, out_ref, rows):
    w = amps_ref.shape[0]
    rows[...] = amps_ref[...].astype(jnp.float32).reshape(w * w, w)
    for d in range(w // 2):
        pair = [rows[pl.ds(2 * d + b, w, stride=w), :] for b in range(2)]
        out_ref[d] = jnp.concatenate(pair, axis=1).astype(jnp.bfloat16)
    for d in range(w // 2, 32):
        out_ref[d] = jnp.zeros((w, 2 * w), jnp.bfloat16)


def near_part(half_ref, rows_ref, factors_ref, total_ref, other_ref, matrix):
    w = rows_ref.shape[1]
    half = half_ref[0]
    first = half == 0
    own = pl.ds(pl.multiple_of(half * 4 * w, 64), 4 * w)
    other = pl.ds(pl.multiple_of((1 - half) * 4 * w, 64), 4 * w)
    mine = jnp.concatenate([factors_ref[p, own, :] for p in range(4)], axis=0)
    for p in range(4):
        other_ref[p] = jnp.where(first, factors_ref[p, :, 4 * w :], factors_ref[p, :, : 4 * w])
    zero = jnp.zeros((4 * w, 4 * w), jnp.bfloat16)
    for b in range(2):
        part = slice(b * w, (b + 1) * w)
        near = jnp.concatenate(
            [jnp.concatenate([rows_ref[y * 8 + k, :, part] for k in range(8)], axis=1) for y in range(4)], axis=0
        )
        across = jnp.where(first, near[:, 4 * w :], near[:, : 4 * w])
        below = -across.astype(jnp.float32).T.astype(jnp.bfloat16)
        matrix[own, :] = near
        matrix[other, :] = jnp.where(
            first, jnp.concatenate([below, zero], axis=1), jnp.concatenate([zero, below], axis=1)
        )
        along = jnp.dot(mine, matrix[...], preferred_element_type=jnp.float32).astype(jnp.bfloat16)
        total = jnp.zeros((4 * w, 8 * w), jnp.float32)
        for p in range(4):
            total += lax.dot_general(
                along[p * 4 * w : (p + 1) * 4 * w], factors_ref[p], LAST, preferred_element_type=jnp.float32
            )
        total_ref[b] = total


def far_part(half_ref, slot_ref, total_ref, far_ref, other_ref, out_ref):
    w = far_ref.shape[0]
    own = pl.ds(pl.multiple_of(half_ref[0] * 4 * w, 64), 4 * w)
    mine = jnp.concatenate([other_ref[p, own, :] for p in range(4)], axis=0)
    zero = jnp.zeros((w, w), jnp.bfloat16)
    results = []
    for b in range(2):
        blocks = {at: far_ref[:, (2 * n + b) * w : (2 * n + b + 1) * w] for n, at in enumerate(UPPER)}
        upper = [[blocks[u, v] if u <= v else zero for v in range(4)] for u in range(4)]
        strict = [[blocks[u, v] if u < v else zero for v in range(4)] for u in range(4)]
        upper, strict = (
            jnp.concatenate([jnp.concatenate(line, axis=1) for line in array], axis=0) for array in (upper, strict)
        )
        along = jnp.dot(mine, upper, preferred_element_type=jnp.float32)
        along -= lax.dot_general(mine, strict, LAST, preferred_element_type=jnp.float32)
        along = along.astype(jnp.bfloat16)
        total = total_ref[b]
        for p in range(4):
            total += lax.dot_general(
                along[p * 4 * w : (p + 1) * 4 * w], other_ref[p], LAST, preferred_element_type=jnp.float32
            )
        results.append(total)
    for y in range(4):
        for k in range(8):
            tile = [r[y * w : (y + 1) * w, k * w : (k + 1) * w] for r in results]
            out_ref[slot_ref[y * 8 + k]] = jnp.concatenate(tile, axis=1).astype(jnp.bfloat16)


def begin(own_ref, bc_ref, amps_ref, shift_a_ref, shift_bc_ref, sum_ref):
    w = amps_ref.shape[0]
    shift_bc = shift_bc_ref[...]
    turned = bc_ref[...].T
    for a in range(w):
        part = slice(a * w, (a + 1) * w)
        ladder = own_ref[:, part].astype(jnp.float32) - turned[part].astype(jnp.float32)
        shift = shift_bc + shift_a_ref[a]
        sum_ref[a] = 2.0 * ladder + shift * amps_ref[a].astype(jnp.float32)


def finish(ab_ref, sum_ref, out_ref):
    w = ab_ref.shape[0]
    twice = 2.0 * ab_ref[...].astype(jnp.float32)
    for a in range(w):
        out_ref[a] = (sum_ref[a] - twice[:, a * w : (a + 1) * w]).astype(jnp.bfloat16)


def on_device(amplitudes, factors, energies):
    w = amplitudes.shape[0]
    half = lax.axis_index("zh")
    index_a = half * 4 + lax.axis_index("y")
    index_b = lax.axis_index("zl")
    index_c = lax.axis_index("x") * 2 + lax.axis_index("core")
    energy_a = lax.dynamic_slice_in_dim(energies, index_a * w, w, 0)
    energy_b = lax.dynamic_slice_in_dim(energies, index_b * w, w, 0)
    energy_c = lax.dynamic_slice_in_dim(energies, index_c * w, w, 0)
    shift_bc = energy_b[:, None] + energy_c[None, :]
    places = np.array([[[slot(h * 4 + y, j, k) for y in range(4) for k in range(8)] for j in range(8)] for h in range(2)])
    places = jnp.asarray(places, jnp.int32)[half, index_b]

    smem = pl.BlockSpec(memory_space=pltpu.SMEM)
    vmem = pl.BlockSpec(memory_space=pltpu.VMEM)
    params = pltpu.CompilerParams(vmem_limit_bytes=40 << 20)
    parts = pl.pallas_call(
        pack,
        out_shape=jax.ShapeDtypeStruct((32, w, 2 * w), jnp.bfloat16),
        in_specs=[vmem],
        out_specs=vmem,
        scratch_shapes=[pltpu.VMEM((w * w, w), jnp.float32)],
        compiler_params=params,
        name="pack",
    )(amplitudes)
    parts = lax.all_to_all(parts, PLANE, split_axis=0, concat_axis=0, tiled=True)
    near = lax.dynamic_slice_in_dim(parts.reshape(4, 8, w, 2 * w), half * 4, 4, 1)
    near = jnp.concatenate([near[u, v] for u, v in UPPER], axis=1)
    far = lax.ppermute(near, "zh", [(0, 1), (1, 0)])
    total, other = pl.pallas_call(
        near_part,
        out_shape=(
            jax.ShapeDtypeStruct((2, 4 * w, 8 * w), jnp.float32),
            jax.ShapeDtypeStruct((4, 8 * w, 4 * w), jnp.bfloat16),
        ),
        in_specs=[smem, vmem, vmem],
        out_specs=(vmem, vmem),
        scratch_shapes=[pltpu.VMEM((8 * w, 8 * w), jnp.bfloat16)],
        compiler_params=params,
        name="near_part",
    )(half.reshape(1), parts, factors)
    close = pl.pallas_call(
        far_part,
        out_shape=jax.ShapeDtypeStruct((32, w, 2 * w), jnp.bfloat16),
        in_specs=[smem, smem, vmem, vmem, vmem],
        out_specs=vmem,
        compiler_params=params,
        name="far_part",
    )(half.reshape(1), places, total, far, other)
    close = lax.all_to_all(close, PLANE, split_axis=0, concat_axis=0, tiled=True)[:24]
    first = close.transpose(1, 0, 2).reshape(w, w * w)
    second = close.reshape(24, w, 2, w).transpose(0, 2, 1, 3).reshape(w, w * w)
    swap_ab = moved(first, lambda i, j, k: (j, i, k))
    swap_bc = moved(second, lambda i, j, k: (i, k, j))
    own = moved(second, lambda i, j, k: (i, j, k))
    partial = pl.pallas_call(
        begin,
        out_shape=jax.ShapeDtypeStruct(amplitudes.shape, jnp.float32),
        in_specs=[vmem, vmem, vmem, smem, vmem],
        out_specs=vmem,
        compiler_params=params,
        name="begin",
    )(own, swap_bc, amplitudes, energy_a, shift_bc)
    return pl.pallas_call(
        finish,
        out_shape=jax.ShapeDtypeStruct(amplitudes.shape, jnp.bfloat16),
        in_specs=[vmem, vmem],
        out_specs=vmem,
        compiler_params=params,
        name="finish",
    )(swap_ab, partial)


def solution(mesh):
    fine = Mesh(mesh.devices.reshape(2, 4, 8, 4, 2), ALL)
    place = P(("zh", "y"), "zl", ("x", "core"))
    return jax.shard_map(on_device, mesh=fine, in_specs=(place, P(), P()), out_specs=place, check_vma=False)
```

```python
import functools

import jax
import jax.numpy as jnp
import numpy as np
from jax import lax
from jax.experimental import pallas as pl
from jax.experimental.pallas import tpu as pltpu
from jax.sharding import Mesh, PartitionSpec as P

ALL = ("zh", "y", "zl", "x", "core")
PLANE = ("y", "x", "core")
UPPER = [(u, v) for u in range(4) for v in range(u, 4)]
LAST = (((1,), (1,)), ((), ()))
MASKS = (389, 85, 114, 41, 49)


def slot(i, j, k):
    bits = k | (i & 3) << 3 | j << 5 | (i >> 2) << 8
    core, x_low, x_high, y_low, y_high = (bin(bits & mask).count("1") & 1 for mask in MASKS)
    return (y_high * 2 + y_low) * 8 + x_high * 4 + x_low * 2 + core


def holder(i, j, k):
    place = slot(i, j, k)
    return (((i >> 2) * 4 + place // 8) * 8 + j) * 8 + place % 8


def moved(array, target):
    pairs = []
    for i in range(8):
        for j in range(8):
            for k in range(8):
                a, b, c = target(i, j, k)
                pairs.append((holder(i, j, k), (a * 8 + b) * 8 + c))
    return lax.ppermute(array, ALL, pairs)


def pack(amps_ref, out_ref, rows):
    w = amps_ref.shape[0]
    rows[...] = amps_ref[...].astype(jnp.float32).reshape(w * w, w)
    for d in range(w // 2):
        pair = [rows[pl.ds(2 * d + b, w, stride=w), :] for b in range(2)]
        out_ref[d] = jnp.concatenate(pair, axis=1).astype(jnp.bfloat16)
    for d in range(w // 2, 32):
        out_ref[d] = jnp.zeros((w, 2 * w), jnp.bfloat16)


def near_part(half_ref, rows_ref, factors_ref, total_ref, other_ref, matrix):
    w = rows_ref.shape[1]
    half = half_ref[0]
    first = half == 0
    own = pl.ds(pl.multiple_of(half * 4 * w, 64), 4 * w)
    other = pl.ds(pl.multiple_of((1 - half) * 4 * w, 64), 4 * w)
    mine = jnp.concatenate([factors_ref[p, own, :] for p in range(4)], axis=0)
    for p in range(4):
        other_ref[p] = jnp.where(first, factors_ref[p, :, 4 * w :], factors_ref[p, :, : 4 * w])
    zero = jnp.zeros((4 * w, 4 * w), jnp.bfloat16)
    for b in range(2):
        part = slice(b * w, (b + 1) * w)
        near = jnp.concatenate(
            [jnp.concatenate([rows_ref[y * 8 + k, :, part] for k in range(8)], axis=1) for y in range(4)], axis=0
        )
        across = jnp.where(first, near[:, 4 * w :], near[:, : 4 * w])
        below = -across.astype(jnp.float32).T.astype(jnp.bfloat16)
        matrix[own, :] = near
        matrix[other, :] = jnp.where(
            first, jnp.concatenate([below, zero], axis=1), jnp.concatenate([zero, below], axis=1)
        )
        along = jnp.dot(mine, matrix[...], preferred_element_type=jnp.float32).astype(jnp.bfloat16)
        total = jnp.zeros((4 * w, 8 * w), jnp.float32)
        for p in range(4):
            total += lax.dot_general(
                along[p * 4 * w : (p + 1) * 4 * w], factors_ref[p], LAST, preferred_element_type=jnp.float32
            )
        total_ref[b] = total


def far_part(half_ref, slot_ref, total_ref, far_ref, other_ref, out_ref):
    w = far_ref.shape[0]
    own = pl.ds(pl.multiple_of(half_ref[0] * 4 * w, 64), 4 * w)
    mine = jnp.concatenate([other_ref[p, own, :] for p in range(4)], axis=0)
    zero = jnp.zeros((w, w), jnp.bfloat16)
    results = []
    for b in range(2):
        blocks = {at: far_ref[:, (2 * n + b) * w : (2 * n + b + 1) * w] for n, at in enumerate(UPPER)}
        upper = [[blocks[u, v] if u <= v else zero for v in range(4)] for u in range(4)]
        strict = [[blocks[u, v] if u < v else zero for v in range(4)] for u in range(4)]
        upper, strict = (
            jnp.concatenate([jnp.concatenate(line, axis=1) for line in array], axis=0) for array in (upper, strict)
        )
        along = jnp.dot(mine, upper, preferred_element_type=jnp.float32)
        along -= lax.dot_general(mine, strict, LAST, preferred_element_type=jnp.float32)
        along = along.astype(jnp.bfloat16)
        total = total_ref[b]
        for p in range(4):
            total += lax.dot_general(
                along[p * 4 * w : (p + 1) * 4 * w], other_ref[p], LAST, preferred_element_type=jnp.float32
            )
        results.append(total)
    for y in range(4):
        for k in range(8):
            tile = [r[y * w : (y + 1) * w, k * w : (k + 1) * w] for r in results]
            out_ref[slot_ref[y * 8 + k]] = jnp.concatenate(tile, axis=1).astype(jnp.bfloat16)


def begin(own_ref, bc_ref, amps_ref, shift_a_ref, shift_bc_ref, sum_ref):
    w = amps_ref.shape[0]
    shift_bc = shift_bc_ref[...]
    turned = bc_ref[...].T
    for a in range(w):
        part = slice(a * w, (a + 1) * w)
        ladder = own_ref[:, part].astype(jnp.float32) - turned[part].astype(jnp.float32)
        shift = shift_bc + shift_a_ref[a]
        sum_ref[a] = 2.0 * ladder + shift * amps_ref[a].astype(jnp.float32)


def finish(ab_ref, sum_ref, out_ref):
    w = ab_ref.shape[0]
    twice = 2.0 * ab_ref[...].astype(jnp.float32)
    for a in range(w):
        out_ref[a] = (sum_ref[a] - twice[:, a * w : (a + 1) * w]).astype(jnp.bfloat16)


def on_device(amplitudes, factors, energies):
    w = amplitudes.shape[0]
    half = lax.axis_index("zh")
    index_a = half * 4 + lax.axis_index("y")
    index_b = lax.axis_index("zl")
    index_c = lax.axis_index("x") * 2 + lax.axis_index("core")
    energy_a = lax.dynamic_slice_in_dim(energies, index_a * w, w, 0)
    energy_b = lax.dynamic_slice_in_dim(energies, index_b * w, w, 0)
    energy_c = lax.dynamic_slice_in_dim(energies, index_c * w, w, 0)
    shift_bc = energy_b[:, None] + energy_c[None, :]
    places = np.array([[[slot(h * 4 + y, j, k) for y in range(4) for k in range(8)] for j in range(8)] for h in range(2)])
    places = jnp.asarray(places, jnp.int32)[half, index_b]

    smem = pl.BlockSpec(memory_space=pltpu.SMEM)
    vmem = pl.BlockSpec(memory_space=pltpu.VMEM)
    params = pltpu.CompilerParams(vmem_limit_bytes=40 << 20)
    parts = pl.pallas_call(
        pack,
        out_shape=jax.ShapeDtypeStruct((32, w, 2 * w), jnp.bfloat16),
        in_specs=[vmem],
        out_specs=vmem,
        scratch_shapes=[pltpu.VMEM((w * w, w), jnp.float32)],
        compiler_params=params,
        name="pack",
    )(amplitudes)
    parts = lax.all_to_all(parts, PLANE, split_axis=0, concat_axis=0, tiled=True)
    near = lax.dynamic_slice_in_dim(parts.reshape(4, 8, w, 2 * w), half * 4, 4, 1)
    near = jnp.concatenate([near[u, v] for u, v in UPPER], axis=1)
    far = lax.ppermute(near, "zh", [(0, 1), (1, 0)])
    total, other = pl.pallas_call(
        near_part,
        out_shape=(
            jax.ShapeDtypeStruct((2, 4 * w, 8 * w), jnp.float32),
            jax.ShapeDtypeStruct((4, 8 * w, 4 * w), jnp.bfloat16),
        ),
        in_specs=[smem, vmem, vmem],
        out_specs=(vmem, vmem),
        scratch_shapes=[pltpu.VMEM((8 * w, 8 * w), jnp.bfloat16)],
        compiler_params=params,
        name="near_part",
    )(half.reshape(1), parts, factors)
    close = pl.pallas_call(
        far_part,
        out_shape=jax.ShapeDtypeStruct((32, w, 2 * w), jnp.bfloat16),
        in_specs=[smem, smem, vmem, vmem, vmem],
        out_specs=vmem,
        compiler_params=params,
        name="far_part",
    )(half.reshape(1), places, total, far, other)
    close = lax.all_to_all(close, PLANE, split_axis=0, concat_axis=0, tiled=True)[:24]
    second = close.reshape(24, w, 2, w).transpose(0, 2, 1, 3).reshape(w, w * w)
    swap_bc = moved(second, lambda i, j, k: (i, k, j))
    first = close.transpose(1, 0, 2).reshape(w, w * w)
    swap_ab = moved(first, lambda i, j, k: (j, i, k))
    third = lax.optimization_barrier(first).reshape(w, w, w).transpose(1, 0, 2).reshape(w, w * w)
    own = moved(third, lambda i, j, k: (i, j, k))
    partial = pl.pallas_call(
        begin,
        out_shape=jax.ShapeDtypeStruct(amplitudes.shape, jnp.float32),
        in_specs=[vmem, vmem, vmem, smem, vmem],
        out_specs=vmem,
        compiler_params=params,
        name="begin",
    )(own, swap_bc, amplitudes, energy_a, shift_bc)
    return pl.pallas_call(
        finish,
        out_shape=jax.ShapeDtypeStruct(amplitudes.shape, jnp.bfloat16),
        in_specs=[vmem, vmem],
        out_specs=vmem,
        compiler_params=params,
        name="finish",
    )(swap_ab, partial)


def solution(mesh):
    fine = Mesh(mesh.devices.reshape(2, 4, 8, 4, 2), ALL)
    place = P(("zh", "y"), "zl", ("x", "core"))
    return jax.shard_map(on_device, mesh=fine, in_specs=(place, P(), P()), out_specs=place, check_vma=False)
```

```python
import functools

import jax
import jax.numpy as jnp
import numpy as np
from jax import lax
from jax.experimental import pallas as pl
from jax.experimental.pallas import tpu as pltpu
from jax.sharding import Mesh, PartitionSpec as P

ALL = ("zh", "y", "zl", "x", "core")
PLANE = ("y", "x", "core")
UPPER = [(u, v) for u in range(4) for v in range(u, 4)]
LAST = (((1,), (1,)), ((), ()))
PLACES = (
    (0, 26, 8, 4, 5, 1, 12, 30, 9, 10, 20, 2, 24, 22, 14, 6, 21, 15, 18, 28, 11, 16, 31, 23, 3, 27, 13, 17, 7, 29, 19, 25),
    (4, 30, 2, 6, 0, 10, 31, 1, 12, 14, 15, 8, 11, 13, 16, 20, 18, 22, 28, 9, 29, 21, 24, 3, 25, 26, 19, 27, 17, 23, 5, 7),
    (2, 24, 28, 0, 30, 6, 10, 12, 8, 31, 11, 20, 13, 4, 3, 14, 22, 16, 17, 18, 23, 19, 21, 25, 7, 1, 29, 15, 26, 27, 5, 9),
    (6, 28, 30, 0, 12, 10, 2, 22, 20, 8, 14, 7, 11, 18, 4, 16, 26, 15, 21, 9, 13, 23, 24, 3, 5, 17, 1, 27, 31, 19, 25, 29),
    (8, 2, 26, 3, 30, 4, 12, 0, 20, 14, 5, 9, 15, 6, 18, 16, 22, 24, 10, 25, 19, 13, 7, 21, 28, 11, 23, 17, 29, 1, 31, 27),
    (16, 0, 4, 22, 18, 12, 24, 26, 10, 14, 15, 8, 2, 9, 11, 20, 28, 3, 1, 27, 19, 30, 23, 13, 17, 5, 6, 29, 31, 7, 25, 21),
    (30, 12, 2, 24, 28, 14, 0, 4, 10, 16, 8, 29, 13, 6, 15, 26, 25, 11, 22, 20, 17, 21, 18, 23, 1, 27, 19, 3, 31, 7, 9, 5),
    (8, 14, 20, 2, 24, 6, 4, 26, 16, 10, 18, 30, 5, 0, 12, 11, 17, 21, 15, 22, 9, 1, 13, 28, 3, 23, 29, 7, 25, 19, 31, 27),
    (30, 12, 6, 2, 26, 4, 0, 18, 20, 3, 7, 8, 10, 1, 24, 13, 31, 25, 16, 27, 5, 22, 14, 21, 15, 28, 19, 17, 23, 9, 29, 11),
    (12, 22, 28, 24, 30, 4, 8, 6, 2, 14, 10, 11, 13, 18, 7, 16, 19, 0, 20, 9, 15, 29, 25, 26, 23, 17, 21, 27, 3, 31, 5, 1),
    (4, 12, 2, 6, 28, 18, 14, 8, 0, 3, 26, 5, 15, 7, 10, 19, 16, 22, 24, 20, 21, 27, 23, 25, 17, 30, 11, 13, 31, 29, 1, 9),
    (24, 14, 28, 2, 8, 9, 20, 4, 15, 12, 0, 10, 21, 16, 13, 6, 22, 26, 3, 7, 11, 17, 18, 25, 5, 27, 1, 30, 23, 19, 29, 31),
    (4, 0, 1, 12, 6, 5, 30, 2, 24, 26, 25, 22, 8, 14, 10, 20, 21, 18, 9, 16, 11, 28, 19, 15, 27, 17, 7, 29, 13, 3, 31, 23),
    (4, 24, 18, 6, 2, 12, 0, 5, 13, 14, 10, 8, 3, 15, 9, 16, 17, 20, 22, 26, 11, 30, 1, 28, 21, 31, 25, 19, 27, 23, 29, 7),
    (6, 26, 4, 28, 12, 7, 14, 0, 13, 8, 18, 9, 22, 10, 15, 2, 27, 29, 19, 16, 20, 24, 23, 21, 17, 30, 31, 1, 25, 3, 11, 5),
    (30, 10, 31, 8, 16, 20, 2, 4, 14, 6, 28, 3, 9, 12, 11, 15, 22, 17, 7, 18, 0, 13, 1, 26, 27, 29, 19, 21, 5, 24, 23, 25),
)


def holder(i, j, k):
    place = PLACES[(i >> 2) * 8 + j][(i & 3) * 8 + k]
    return (((i >> 2) * 4 + place // 8) * 8 + j) * 8 + place % 8


def moved(array, target):
    pairs = []
    for i in range(8):
        for j in range(8):
            for k in range(8):
                a, b, c = target(i, j, k)
                pairs.append((holder(i, j, k), (a * 8 + b) * 8 + c))
    return lax.ppermute(array, ALL, pairs)


def pack(amps_ref, out_ref, rows):
    w = amps_ref.shape[0]
    rows[...] = amps_ref[...].astype(jnp.float32).reshape(w * w, w)
    for d in range(w // 2):
        pair = [rows[pl.ds(2 * d + b, w, stride=w), :] for b in range(2)]
        out_ref[d] = jnp.concatenate(pair, axis=1).astype(jnp.bfloat16)
    for d in range(w // 2, 32):
        out_ref[d] = jnp.zeros((w, 2 * w), jnp.bfloat16)


def near_part(half_ref, rows_ref, factors_ref, total_ref, other_ref, matrix):
    w = rows_ref.shape[1]
    half = half_ref[0]
    first = half == 0
    own = pl.ds(pl.multiple_of(half * 4 * w, 64), 4 * w)
    other = pl.ds(pl.multiple_of((1 - half) * 4 * w, 64), 4 * w)
    mine = jnp.concatenate([factors_ref[p, own, :] for p in range(4)], axis=0)
    for p in range(4):
        other_ref[p] = jnp.where(first, factors_ref[p, :, 4 * w :], factors_ref[p, :, : 4 * w])
    zero = jnp.zeros((4 * w, 4 * w), jnp.bfloat16)
    for b in range(2):
        part = slice(b * w, (b + 1) * w)
        near = jnp.concatenate(
            [jnp.concatenate([rows_ref[y * 8 + k, :, part] for k in range(8)], axis=1) for y in range(4)], axis=0
        )
        across = jnp.where(first, near[:, 4 * w :], near[:, : 4 * w])
        below = -across.astype(jnp.float32).T.astype(jnp.bfloat16)
        matrix[own, :] = near
        matrix[other, :] = jnp.where(
            first, jnp.concatenate([below, zero], axis=1), jnp.concatenate([zero, below], axis=1)
        )
        along = jnp.dot(mine, matrix[...], preferred_element_type=jnp.float32).astype(jnp.bfloat16)
        total = jnp.zeros((4 * w, 8 * w), jnp.float32)
        for p in range(4):
            total += lax.dot_general(
                along[p * 4 * w : (p + 1) * 4 * w], factors_ref[p], LAST, preferred_element_type=jnp.float32
            )
        total_ref[b] = total


def far_part(half_ref, slot_ref, total_ref, far_ref, other_ref, out_ref):
    w = far_ref.shape[0]
    own = pl.ds(pl.multiple_of(half_ref[0] * 4 * w, 64), 4 * w)
    mine = jnp.concatenate([other_ref[p, own, :] for p in range(4)], axis=0)
    zero = jnp.zeros((w, w), jnp.bfloat16)
    results = []
    for b in range(2):
        blocks = {at: far_ref[:, (2 * n + b) * w : (2 * n + b + 1) * w] for n, at in enumerate(UPPER)}
        upper = [[blocks[u, v] if u <= v else zero for v in range(4)] for u in range(4)]
        strict = [[blocks[u, v] if u < v else zero for v in range(4)] for u in range(4)]
        upper, strict = (
            jnp.concatenate([jnp.concatenate(line, axis=1) for line in array], axis=0) for array in (upper, strict)
        )
        along = jnp.dot(mine, upper, preferred_element_type=jnp.float32)
        along -= lax.dot_general(mine, strict, LAST, preferred_element_type=jnp.float32)
        along = along.astype(jnp.bfloat16)
        total = total_ref[b]
        for p in range(4):
            total += lax.dot_general(
                along[p * 4 * w : (p + 1) * 4 * w], other_ref[p], LAST, preferred_element_type=jnp.float32
            )
        results.append(total)
    for y in range(4):
        for k in range(8):
            tile = [r[y * w : (y + 1) * w, k * w : (k + 1) * w] for r in results]
            out_ref[slot_ref[y * 8 + k]] = jnp.concatenate(tile, axis=1).astype(jnp.bfloat16)


def begin(own_ref, bc_ref, amps_ref, shift_a_ref, shift_bc_ref, sum_ref, own_rows, bc_rows):
    w = amps_ref.shape[0]
    shift_bc = shift_bc_ref[...]
    for n in range(w):
        part = slice(n * w, (n + 1) * w)
        own_rows[pl.ds(n, w, stride=w), :] = own_ref[:, part].astype(jnp.float32)
        bc_rows[pl.ds(n, w, stride=w), :] = bc_ref[:, part].astype(jnp.float32)
    turned = bc_rows[...].T
    for a in range(w):
        part = slice(a * w, (a + 1) * w)
        ladder = own_rows[part, :] - turned[:, part]
        shift = shift_bc + shift_a_ref[a]
        sum_ref[a] = 2.0 * ladder + shift * amps_ref[a].astype(jnp.float32)


def finish(ab_ref, sum_ref, out_ref):
    w = ab_ref.shape[0]
    twice = 2.0 * ab_ref[...].astype(jnp.float32)
    for a in range(w):
        out_ref[a] = (sum_ref[a] - twice[:, a * w : (a + 1) * w]).astype(jnp.bfloat16)


def on_device(amplitudes, factors, energies):
    w = amplitudes.shape[0]
    half = lax.axis_index("zh")
    index_a = half * 4 + lax.axis_index("y")
    index_b = lax.axis_index("zl")
    index_c = lax.axis_index("x") * 2 + lax.axis_index("core")
    energy_a = lax.dynamic_slice_in_dim(energies, index_a * w, w, 0)
    energy_b = lax.dynamic_slice_in_dim(energies, index_b * w, w, 0)
    energy_c = lax.dynamic_slice_in_dim(energies, index_c * w, w, 0)
    shift_bc = energy_b[:, None] + energy_c[None, :]
    places = jnp.asarray(np.array(PLACES), jnp.int32)[half * 8 + index_b]

    smem = pl.BlockSpec(memory_space=pltpu.SMEM)
    vmem = pl.BlockSpec(memory_space=pltpu.VMEM)
    params = pltpu.CompilerParams(vmem_limit_bytes=40 << 20)
    parts = pl.pallas_call(
        pack,
        out_shape=jax.ShapeDtypeStruct((32, w, 2 * w), jnp.bfloat16),
        in_specs=[vmem],
        out_specs=vmem,
        scratch_shapes=[pltpu.VMEM((w * w, w), jnp.float32)],
        compiler_params=params,
        name="pack",
    )(amplitudes)
    parts = lax.all_to_all(parts, PLANE, split_axis=0, concat_axis=0, tiled=True)
    near = lax.dynamic_slice_in_dim(parts.reshape(4, 8, w, 2 * w), half * 4, 4, 1)
    near = jnp.concatenate([near[u, v] for u, v in UPPER], axis=1)
    far = lax.ppermute(near, "zh", [(0, 1), (1, 0)])
    total, other = pl.pallas_call(
        near_part,
        out_shape=(
            jax.ShapeDtypeStruct((2, 4 * w, 8 * w), jnp.float32),
            jax.ShapeDtypeStruct((4, 8 * w, 4 * w), jnp.bfloat16),
        ),
        in_specs=[smem, vmem, vmem],
        out_specs=(vmem, vmem),
        scratch_shapes=[pltpu.VMEM((8 * w, 8 * w), jnp.bfloat16)],
        compiler_params=params,
        name="near_part",
    )(half.reshape(1), parts, factors)
    close = pl.pallas_call(
        far_part,
        out_shape=jax.ShapeDtypeStruct((32, w, 2 * w), jnp.bfloat16),
        in_specs=[smem, smem, vmem, vmem, vmem],
        out_specs=vmem,
        compiler_params=params,
        name="far_part",
    )(half.reshape(1), places, total, far, other)
    close = lax.all_to_all(close, PLANE, split_axis=0, concat_axis=0, tiled=True)[:24]
    first = close.transpose(1, 0, 2).reshape(w, w * w)
    swap_ab = moved(first, lambda i, j, k: (j, i, k))
    swap_bc = moved(first, lambda i, j, k: (i, k, j))
    own = moved(first, lambda i, j, k: (i, j, k))
    partial = pl.pallas_call(
        begin,
        out_shape=jax.ShapeDtypeStruct(amplitudes.shape, jnp.float32),
        in_specs=[vmem, vmem, vmem, smem, vmem],
        out_specs=vmem,
        scratch_shapes=[pltpu.VMEM((w * w, w), jnp.float32)] * 2,
        compiler_params=params,
        name="begin",
    )(own, swap_bc, amplitudes, energy_a, shift_bc)
    return pl.pallas_call(
        finish,
        out_shape=jax.ShapeDtypeStruct(amplitudes.shape, jnp.bfloat16),
        in_specs=[vmem, vmem],
        out_specs=vmem,
        compiler_params=params,
        name="finish",
    )(swap_ab, partial)


def solution(mesh):
    fine = Mesh(mesh.devices.reshape(2, 4, 8, 4, 2), ALL)
    place = P(("zh", "y"), "zl", ("x", "core"))
    return jax.shard_map(on_device, mesh=fine, in_specs=(place, P(), P()), out_specs=place, check_vma=False)
```

```python
import functools

import jax
import jax.numpy as jnp
import numpy as np
from jax import lax
from jax.experimental import pallas as pl
from jax.experimental.pallas import tpu as pltpu
from jax.sharding import Mesh, PartitionSpec as P

ALL = ("zh", "y", "zl", "x", "core")
PLANE = ("y", "x", "core")
UPPER = [(u, v) for u in range(4) for v in range(u, 4)]
LAST = (((1,), (1,)), ((), ()))
PLACES = (
    (0, 26, 8, 4, 5, 1, 12, 30, 9, 10, 20, 2, 24, 22, 14, 6, 21, 15, 18, 28, 11, 16, 31, 23, 3, 27, 13, 17, 7, 29, 19, 25),
    (4, 30, 2, 6, 0, 10, 31, 1, 12, 14, 15, 8, 11, 13, 16, 20, 18, 22, 28, 9, 29, 21, 24, 3, 25, 26, 19, 27, 17, 23, 5, 7),
    (2, 24, 28, 0, 30, 6, 10, 12, 8, 31, 11, 20, 13, 4, 3, 14, 22, 16, 17, 18, 23, 19, 21, 25, 7, 1, 29, 15, 26, 27, 5, 9),
    (6, 28, 30, 0, 12, 10, 2, 22, 20, 8, 14, 7, 11, 18, 4, 16, 26, 15, 21, 9, 13, 23, 24, 3, 5, 17, 1, 27, 31, 19, 25, 29),
    (8, 2, 26, 3, 30, 4, 12, 0, 20, 14, 5, 9, 15, 6, 18, 16, 22, 24, 10, 25, 19, 13, 7, 21, 28, 11, 23, 17, 29, 1, 31, 27),
    (16, 0, 4, 22, 18, 12, 24, 26, 10, 14, 15, 8, 2, 9, 11, 20, 28, 3, 1, 27, 19, 30, 23, 13, 17, 5, 6, 29, 31, 7, 25, 21),
    (30, 12, 2, 24, 28, 14, 0, 4, 10, 16, 8, 29, 13, 6, 15, 26, 25, 11, 22, 20, 17, 21, 18, 23, 1, 27, 19, 3, 31, 7, 9, 5),
    (8, 14, 20, 2, 24, 6, 4, 26, 16, 10, 18, 30, 5, 0, 12, 11, 17, 21, 15, 22, 9, 1, 13, 28, 3, 23, 29, 7, 25, 19, 31, 27),
    (30, 12, 6, 2, 26, 4, 0, 18, 20, 3, 7, 8, 10, 1, 24, 13, 31, 25, 16, 27, 5, 22, 14, 21, 15, 28, 19, 17, 23, 9, 29, 11),
    (12, 22, 28, 24, 30, 4, 8, 6, 2, 14, 10, 11, 13, 18, 7, 16, 19, 0, 20, 9, 15, 29, 25, 26, 23, 17, 21, 27, 3, 31, 5, 1),
    (4, 12, 2, 6, 28, 18, 14, 8, 0, 3, 26, 5, 15, 7, 10, 19, 16, 22, 24, 20, 21, 27, 23, 25, 17, 30, 11, 13, 31, 29, 1, 9),
    (24, 14, 28, 2, 8, 9, 20, 4, 15, 12, 0, 10, 21, 16, 13, 6, 22, 26, 3, 7, 11, 17, 18, 25, 5, 27, 1, 30, 23, 19, 29, 31),
    (4, 0, 1, 12, 6, 5, 30, 2, 24, 26, 25, 22, 8, 14, 10, 20, 21, 18, 9, 16, 11, 28, 19, 15, 27, 17, 7, 29, 13, 3, 31, 23),
    (4, 24, 18, 6, 2, 12, 0, 5, 13, 14, 10, 8, 3, 15, 9, 16, 17, 20, 22, 26, 11, 30, 1, 28, 21, 31, 25, 19, 27, 23, 29, 7),
    (6, 26, 4, 28, 12, 7, 14, 0, 13, 8, 18, 9, 22, 10, 15, 2, 27, 29, 19, 16, 20, 24, 23, 21, 17, 30, 31, 1, 25, 3, 11, 5),
    (30, 10, 31, 8, 16, 20, 2, 4, 14, 6, 28, 3, 9, 12, 11, 15, 22, 17, 7, 18, 0, 13, 1, 26, 27, 29, 19, 21, 5, 24, 23, 25),
)


def holder(i, j, k):
    place = PLACES[(i >> 2) * 8 + j][(i & 3) * 8 + k]
    return (((i >> 2) * 4 + place // 8) * 8 + j) * 8 + place % 8


def moved(array, target):
    pairs = []
    for i in range(8):
        for j in range(8):
            for k in range(8):
                a, b, c = target(i, j, k)
                pairs.append((holder(i, j, k), (a * 8 + b) * 8 + c))
    return lax.ppermute(array, ALL, pairs)


def pack(amps_ref, out_ref, rows):
    w = amps_ref.shape[0]
    rows[...] = amps_ref[...].astype(jnp.float32).reshape(w * w, w)
    for d in range(w // 2):
        pair = [rows[pl.ds(2 * d + b, w, stride=w), :] for b in range(2)]
        out_ref[d] = jnp.concatenate(pair, axis=1).astype(jnp.bfloat16)
    for d in range(w // 2, 32):
        out_ref[d] = jnp.zeros((w, 2 * w), jnp.bfloat16)


def near_part(half_ref, rows_ref, factors_ref, total_ref, other_ref, matrix):
    w = rows_ref.shape[1]
    half = half_ref[0]
    first = half == 0
    own = pl.ds(pl.multiple_of(half * 4 * w, 64), 4 * w)
    other = pl.ds(pl.multiple_of((1 - half) * 4 * w, 64), 4 * w)
    mine = jnp.concatenate([factors_ref[p, own, :] for p in range(4)], axis=0)
    for p in range(4):
        other_ref[p] = jnp.where(first, factors_ref[p, :, 4 * w :], factors_ref[p, :, : 4 * w])
    zero = jnp.zeros((4 * w, 4 * w), jnp.bfloat16)
    for b in range(2):
        part = slice(b * w, (b + 1) * w)
        near = jnp.concatenate(
            [jnp.concatenate([rows_ref[y * 8 + k, :, part] for k in range(8)], axis=1) for y in range(4)], axis=0
        )
        across = jnp.where(first, near[:, 4 * w :], near[:, : 4 * w])
        below = -across.astype(jnp.float32).T.astype(jnp.bfloat16)
        matrix[own, :] = near
        matrix[other, :] = jnp.where(
            first, jnp.concatenate([below, zero], axis=1), jnp.concatenate([zero, below], axis=1)
        )
        along = jnp.dot(mine, matrix[...], preferred_element_type=jnp.float32).astype(jnp.bfloat16)
        total = jnp.zeros((4 * w, 8 * w), jnp.float32)
        for p in range(4):
            total += lax.dot_general(
                along[p * 4 * w : (p + 1) * 4 * w], factors_ref[p], LAST, preferred_element_type=jnp.float32
            )
        total_ref[b] = total


def far_part(half_ref, slot_ref, total_ref, far_ref, other_ref, out_ref):
    w = far_ref.shape[0]
    own = pl.ds(pl.multiple_of(half_ref[0] * 4 * w, 64), 4 * w)
    mine = jnp.concatenate([other_ref[p, own, :] for p in range(4)], axis=0)
    zero = jnp.zeros((w, w), jnp.bfloat16)
    results = []
    for b in range(2):
        blocks = {at: far_ref[:, (2 * n + b) * w : (2 * n + b + 1) * w] for n, at in enumerate(UPPER)}
        upper = [[blocks[u, v] if u <= v else zero for v in range(4)] for u in range(4)]
        strict = [[blocks[u, v] if u < v else zero for v in range(4)] for u in range(4)]
        upper, strict = (
            jnp.concatenate([jnp.concatenate(line, axis=1) for line in array], axis=0) for array in (upper, strict)
        )
        along = jnp.dot(mine, upper, preferred_element_type=jnp.float32)
        along -= lax.dot_general(mine, strict, LAST, preferred_element_type=jnp.float32)
        along = along.astype(jnp.bfloat16)
        total = total_ref[b]
        for p in range(4):
            total += lax.dot_general(
                along[p * 4 * w : (p + 1) * 4 * w], other_ref[p], LAST, preferred_element_type=jnp.float32
            )
        results.append(total)
    for y in range(4):
        for k in range(8):
            tile = [r[y * w : (y + 1) * w, k * w : (k + 1) * w] for r in results]
            out_ref[slot_ref[y * 8 + k]] = jnp.concatenate(tile, axis=1).astype(jnp.bfloat16)


def begin(bc_ref, amps_ref, shift_a_ref, shift_bc_ref, sum_ref, rows):
    w = amps_ref.shape[0]
    shift_bc = shift_bc_ref[...]
    for n in range(w):
        rows[pl.ds(n, w, stride=w), :] = bc_ref[:, n * w : (n + 1) * w].astype(jnp.float32)
    turned = rows[...].T
    for a in range(w):
        shift = shift_bc + shift_a_ref[a]
        sum_ref[a] = shift * amps_ref[a].astype(jnp.float32) - 2.0 * turned[:, a * w : (a + 1) * w]


def finish(own_ref, ab_ref, sum_ref, out_ref, rows):
    w = ab_ref.shape[0]
    for n in range(w):
        rows[pl.ds(n, w, stride=w), :] = own_ref[:, n * w : (n + 1) * w].astype(jnp.float32)
    for a in range(w):
        part = slice(a * w, (a + 1) * w)
        ladder = rows[part, :] - ab_ref[:, part].astype(jnp.float32)
        out_ref[a] = (sum_ref[a] + 2.0 * ladder).astype(jnp.bfloat16)


def on_device(amplitudes, factors, energies):
    w = amplitudes.shape[0]
    half = lax.axis_index("zh")
    index_a = half * 4 + lax.axis_index("y")
    index_b = lax.axis_index("zl")
    index_c = lax.axis_index("x") * 2 + lax.axis_index("core")
    energy_a = lax.dynamic_slice_in_dim(energies, index_a * w, w, 0)
    energy_b = lax.dynamic_slice_in_dim(energies, index_b * w, w, 0)
    energy_c = lax.dynamic_slice_in_dim(energies, index_c * w, w, 0)
    shift_bc = energy_b[:, None] + energy_c[None, :]
    places = jnp.asarray(np.array(PLACES), jnp.int32)[half * 8 + index_b]

    smem = pl.BlockSpec(memory_space=pltpu.SMEM)
    vmem = pl.BlockSpec(memory_space=pltpu.VMEM)
    params = pltpu.CompilerParams(vmem_limit_bytes=40 << 20)
    parts = pl.pallas_call(
        pack,
        out_shape=jax.ShapeDtypeStruct((32, w, 2 * w), jnp.bfloat16),
        in_specs=[vmem],
        out_specs=vmem,
        scratch_shapes=[pltpu.VMEM((w * w, w), jnp.float32)],
        compiler_params=params,
        name="pack",
    )(amplitudes)
    parts = lax.all_to_all(parts, PLANE, split_axis=0, concat_axis=0, tiled=True)
    near = lax.dynamic_slice_in_dim(parts.reshape(4, 8, w, 2 * w), half * 4, 4, 1)
    near = jnp.concatenate([near[u, v] for u, v in UPPER], axis=1)
    far = lax.ppermute(near, "zh", [(0, 1), (1, 0)])
    total, other = pl.pallas_call(
        near_part,
        out_shape=(
            jax.ShapeDtypeStruct((2, 4 * w, 8 * w), jnp.float32),
            jax.ShapeDtypeStruct((4, 8 * w, 4 * w), jnp.bfloat16),
        ),
        in_specs=[smem, vmem, vmem],
        out_specs=(vmem, vmem),
        scratch_shapes=[pltpu.VMEM((8 * w, 8 * w), jnp.bfloat16)],
        compiler_params=params,
        name="near_part",
    )(half.reshape(1), parts, factors)
    close = pl.pallas_call(
        far_part,
        out_shape=jax.ShapeDtypeStruct((32, w, 2 * w), jnp.bfloat16),
        in_specs=[smem, smem, vmem, vmem, vmem],
        out_specs=vmem,
        compiler_params=params,
        name="far_part",
    )(half.reshape(1), places, total, far, other)
    close = lax.all_to_all(close, PLANE, split_axis=0, concat_axis=0, tiled=True)[:24]
    first = close.transpose(1, 0, 2).reshape(w, w * w)
    swap_ab = moved(first, lambda i, j, k: (j, i, k))
    swap_bc = moved(first, lambda i, j, k: (i, k, j))
    own = moved(first, lambda i, j, k: (i, j, k))
    partial = pl.pallas_call(
        begin,
        out_shape=jax.ShapeDtypeStruct(amplitudes.shape, jnp.float32),
        in_specs=[vmem, vmem, smem, vmem],
        out_specs=vmem,
        scratch_shapes=[pltpu.VMEM((w * w, w), jnp.float32)],
        compiler_params=params,
        name="begin",
    )(swap_bc, amplitudes, energy_a, shift_bc)
    return pl.pallas_call(
        finish,
        out_shape=jax.ShapeDtypeStruct(amplitudes.shape, jnp.bfloat16),
        in_specs=[vmem, vmem, vmem],
        out_specs=vmem,
        scratch_shapes=[pltpu.VMEM((w * w, w), jnp.float32)],
        compiler_params=params,
        name="finish",
    )(own, swap_ab, partial)


def solution(mesh):
    fine = Mesh(mesh.devices.reshape(2, 4, 8, 4, 2), ALL)
    place = P(("zh", "y"), "zl", ("x", "core"))
    return jax.shard_map(on_device, mesh=fine, in_specs=(place, P(), P()), out_specs=place, check_vma=False)
```

```python
import functools

import jax
import jax.numpy as jnp
import numpy as np
from jax import lax
from jax.experimental import pallas as pl
from jax.experimental.pallas import tpu as pltpu
from jax.sharding import Mesh, PartitionSpec as P

ALL = ("zh", "y", "zl", "x", "core")
PLANE = ("y", "x", "core")
UPPER = [(u, v) for u in range(4) for v in range(u + 1, 4)]
LAST = (((1,), (1,)), ((), ()))
PLACES = (
    (0, 26, 8, 4, 5, 1, 12, 30, 9, 10, 20, 2, 24, 22, 14, 6, 21, 15, 18, 28, 11, 16, 31, 23, 3, 27, 13, 17, 7, 29, 19, 25),
    (4, 30, 2, 6, 0, 10, 31, 1, 12, 14, 15, 8, 11, 13, 16, 20, 18, 22, 28, 9, 29, 21, 24, 3, 25, 26, 19, 27, 17, 23, 5, 7),
    (2, 24, 28, 0, 30, 6, 10, 12, 8, 31, 11, 20, 13, 4, 3, 14, 22, 16, 17, 18, 23, 19, 21, 25, 7, 1, 29, 15, 26, 27, 5, 9),
    (6, 28, 30, 0, 12, 10, 2, 22, 20, 8, 14, 7, 11, 18, 4, 16, 26, 15, 21, 9, 13, 23, 24, 3, 5, 17, 1, 27, 31, 19, 25, 29),
    (8, 2, 26, 3, 30, 4, 12, 0, 20, 14, 5, 9, 15, 6, 18, 16, 22, 24, 10, 25, 19, 13, 7, 21, 28, 11, 23, 17, 29, 1, 31, 27),
    (16, 0, 4, 22, 18, 12, 24, 26, 10, 14, 15, 8, 2, 9, 11, 20, 28, 3, 1, 27, 19, 30, 23, 13, 17, 5, 6, 29, 31, 7, 25, 21),
    (30, 12, 2, 24, 28, 14, 0, 4, 10, 16, 8, 29, 13, 6, 15, 26, 25, 11, 22, 20, 17, 21, 18, 23, 1, 27, 19, 3, 31, 7, 9, 5),
    (8, 14, 20, 2, 24, 6, 4, 26, 16, 10, 18, 30, 5, 0, 12, 11, 17, 21, 15, 22, 9, 1, 13, 28, 3, 23, 29, 7, 25, 19, 31, 27),
    (30, 12, 6, 2, 26, 4, 0, 18, 20, 3, 7, 8, 10, 1, 24, 13, 31, 25, 16, 27, 5, 22, 14, 21, 15, 28, 19, 17, 23, 9, 29, 11),
    (12, 22, 28, 24, 30, 4, 8, 6, 2, 14, 10, 11, 13, 18, 7, 16, 19, 0, 20, 9, 15, 29, 25, 26, 23, 17, 21, 27, 3, 31, 5, 1),
    (4, 12, 2, 6, 28, 18, 14, 8, 0, 3, 26, 5, 15, 7, 10, 19, 16, 22, 24, 20, 21, 27, 23, 25, 17, 30, 11, 13, 31, 29, 1, 9),
    (24, 14, 28, 2, 8, 9, 20, 4, 15, 12, 0, 10, 21, 16, 13, 6, 22, 26, 3, 7, 11, 17, 18, 25, 5, 27, 1, 30, 23, 19, 29, 31),
    (4, 0, 1, 12, 6, 5, 30, 2, 24, 26, 25, 22, 8, 14, 10, 20, 21, 18, 9, 16, 11, 28, 19, 15, 27, 17, 7, 29, 13, 3, 31, 23),
    (4, 24, 18, 6, 2, 12, 0, 5, 13, 14, 10, 8, 3, 15, 9, 16, 17, 20, 22, 26, 11, 30, 1, 28, 21, 31, 25, 19, 27, 23, 29, 7),
    (6, 26, 4, 28, 12, 7, 14, 0, 13, 8, 18, 9, 22, 10, 15, 2, 27, 29, 19, 16, 20, 24, 23, 21, 17, 30, 31, 1, 25, 3, 11, 5),
    (30, 10, 31, 8, 16, 20, 2, 4, 14, 6, 28, 3, 9, 12, 11, 15, 22, 17, 7, 18, 0, 13, 1, 26, 27, 29, 19, 21, 5, 24, 23, 25),
)


def holder(i, j, k):
    place = PLACES[(i >> 2) * 8 + j][(i & 3) * 8 + k]
    return (((i >> 2) * 4 + place // 8) * 8 + j) * 8 + place % 8


def moved(array, target):
    pairs = []
    for i in range(8):
        for j in range(8):
            for k in range(8):
                a, b, c = target(i, j, k)
                pairs.append((holder(i, j, k), (a * 8 + b) * 8 + c))
    return lax.ppermute(array, ALL, pairs)


def pack(amps_ref, out_ref, rows):
    w = amps_ref.shape[0]
    rows[...] = amps_ref[...].astype(jnp.float32).reshape(w * w, w)
    for d in range(w // 2):
        pair = [rows[pl.ds(2 * d + b, w, stride=w), :] for b in range(2)]
        out_ref[d] = jnp.concatenate(pair, axis=1).astype(jnp.bfloat16)
    for d in range(w // 2, 32):
        out_ref[d] = jnp.zeros((w, 2 * w), jnp.bfloat16)


def near_part(half_ref, rows_ref, factors_ref, total_ref, other_ref, matrix):
    w = rows_ref.shape[1]
    half = half_ref[0]
    first = half == 0
    own = pl.ds(pl.multiple_of(half * 4 * w, 64), 4 * w)
    other = pl.ds(pl.multiple_of((1 - half) * 4 * w, 64), 4 * w)
    mine = jnp.concatenate([factors_ref[p, own, :] for p in range(4)], axis=0)
    for p in range(4):
        other_ref[p] = jnp.where(first, factors_ref[p, :, 4 * w :], factors_ref[p, :, : 4 * w])
    zero = jnp.zeros((4 * w, 4 * w), jnp.bfloat16)
    for b in range(2):
        part = slice(b * w, (b + 1) * w)
        near = jnp.concatenate(
            [jnp.concatenate([rows_ref[y * 8 + k, :, part] for k in range(8)], axis=1) for y in range(4)], axis=0
        )
        across = jnp.where(first, near[:, 4 * w :], near[:, : 4 * w])
        below = -across.astype(jnp.float32).T.astype(jnp.bfloat16)
        matrix[own, :] = near
        matrix[other, :] = jnp.where(
            first, jnp.concatenate([below, zero], axis=1), jnp.concatenate([zero, below], axis=1)
        )
        along = jnp.dot(mine, matrix[...], preferred_element_type=jnp.float32).astype(jnp.bfloat16)
        total = jnp.zeros((4 * w, 8 * w), jnp.float32)
        for p in range(4):
            total += lax.dot_general(
                along[p * 4 * w : (p + 1) * 4 * w], factors_ref[p], LAST, preferred_element_type=jnp.float32
            )
        total_ref[b] = total


def far_part(half_ref, slot_ref, total_ref, far_ref, other_ref, out_ref):
    w = far_ref.shape[0]
    own = pl.ds(pl.multiple_of(half_ref[0] * 4 * w, 64), 4 * w)
    mine = jnp.concatenate([other_ref[p, own, :] for p in range(4)], axis=0)
    zero = jnp.zeros((w, w), jnp.float32)
    row = lax.broadcasted_iota(jnp.int32, (w, w), 0)
    column = lax.broadcasted_iota(jnp.int32, (w, w), 1)
    results = []
    for b in range(2):
        blocks = [far_ref[:, (2 * n + b) * w : (2 * n + b + 1) * w].astype(jnp.float32) for n in range(8)]
        found = dict(zip(UPPER, blocks))
        for n in range(2):
            found[2 * n, 2 * n] = jnp.where(row < column, blocks[6 + n], zero)
            found[2 * n + 1, 2 * n + 1] = jnp.where(row > column, blocks[6 + n], zero)
        part = [jnp.concatenate([found.get((u, v), zero) for v in range(4)], axis=1) for u in range(4)]
        part = jnp.concatenate(part, axis=0).astype(jnp.bfloat16)
        along = jnp.dot(mine, part, preferred_element_type=jnp.float32)
        along -= lax.dot_general(mine, part, LAST, preferred_element_type=jnp.float32)
        along = along.astype(jnp.bfloat16)
        total = total_ref[b]
        for p in range(4):
            total += lax.dot_general(
                along[p * 4 * w : (p + 1) * 4 * w], other_ref[p], LAST, preferred_element_type=jnp.float32
            )
        results.append(total)
    for y in range(4):
        for k in range(8):
            tile = [r[y * w : (y + 1) * w, k * w : (k + 1) * w] for r in results]
            out_ref[slot_ref[y * 8 + k]] = jnp.concatenate(tile, axis=1).astype(jnp.bfloat16)


def begin(bc_ref, amps_ref, shift_a_ref, shift_bc_ref, sum_ref, rows):
    w = amps_ref.shape[0]
    shift_bc = shift_bc_ref[...]
    for n in range(w):
        rows[pl.ds(n, w, stride=w), :] = bc_ref[:, n * w : (n + 1) * w].astype(jnp.float32)
    turned = rows[...].T
    for a in range(w):
        shift = shift_bc + shift_a_ref[a]
        sum_ref[a] = shift * amps_ref[a].astype(jnp.float32) - 2.0 * turned[:, a * w : (a + 1) * w]


def finish(own_ref, ab_ref, sum_ref, out_ref, rows):
    w = ab_ref.shape[0]
    for n in range(w):
        rows[pl.ds(n, w, stride=w), :] = own_ref[:, n * w : (n + 1) * w].astype(jnp.float32)
    for a in range(w):
        part = slice(a * w, (a + 1) * w)
        ladder = rows[part, :] - ab_ref[:, part].astype(jnp.float32)
        out_ref[a] = (sum_ref[a] + 2.0 * ladder).astype(jnp.bfloat16)


def on_device(amplitudes, factors, energies):
    w = amplitudes.shape[0]
    half = lax.axis_index("zh")
    index_a = half * 4 + lax.axis_index("y")
    index_b = lax.axis_index("zl")
    index_c = lax.axis_index("x") * 2 + lax.axis_index("core")
    energy_a = lax.dynamic_slice_in_dim(energies, index_a * w, w, 0)
    energy_b = lax.dynamic_slice_in_dim(energies, index_b * w, w, 0)
    energy_c = lax.dynamic_slice_in_dim(energies, index_c * w, w, 0)
    shift_bc = energy_b[:, None] + energy_c[None, :]
    places = jnp.asarray(np.array(PLACES), jnp.int32)[half * 8 + index_b]

    smem = pl.BlockSpec(memory_space=pltpu.SMEM)
    vmem = pl.BlockSpec(memory_space=pltpu.VMEM)
    params = pltpu.CompilerParams(vmem_limit_bytes=40 << 20)
    parts = pl.pallas_call(
        pack,
        out_shape=jax.ShapeDtypeStruct((32, w, 2 * w), jnp.bfloat16),
        in_specs=[vmem],
        out_specs=vmem,
        scratch_shapes=[pltpu.VMEM((w * w, w), jnp.float32)],
        compiler_params=params,
        name="pack",
    )(amplitudes)
    parts = lax.all_to_all(parts, PLANE, split_axis=0, concat_axis=0, tiled=True)
    near = lax.dynamic_slice_in_dim(parts.reshape(4, 8, w, 2 * w), half * 4, 4, 1)
    above = np.arange(w)[:, None] < np.arange(2 * w)[None, :] % w
    mixed = [jnp.where(above, near[2 * n, 2 * n], near[2 * n + 1, 2 * n + 1]) for n in range(2)]
    near = jnp.concatenate([near[u, v] for u, v in UPPER] + mixed, axis=1)
    far = lax.ppermute(near, "zh", [(0, 1), (1, 0)])
    total, other = pl.pallas_call(
        near_part,
        out_shape=(
            jax.ShapeDtypeStruct((2, 4 * w, 8 * w), jnp.float32),
            jax.ShapeDtypeStruct((4, 8 * w, 4 * w), jnp.bfloat16),
        ),
        in_specs=[smem, vmem, vmem],
        out_specs=(vmem, vmem),
        scratch_shapes=[pltpu.VMEM((8 * w, 8 * w), jnp.bfloat16)],
        compiler_params=params,
        name="near_part",
    )(half.reshape(1), parts, factors)
    close = pl.pallas_call(
        far_part,
        out_shape=jax.ShapeDtypeStruct((32, w, 2 * w), jnp.bfloat16),
        in_specs=[smem, smem, vmem, vmem, vmem],
        out_specs=vmem,
        compiler_params=params,
        name="far_part",
    )(half.reshape(1), places, total, far, other)
    close = lax.all_to_all(close, PLANE, split_axis=0, concat_axis=0, tiled=True)[:24]
    first = close.transpose(1, 0, 2).reshape(w, w * w)
    swap_ab = moved(first, lambda i, j, k: (j, i, k))
    swap_bc = moved(first, lambda i, j, k: (i, k, j))
    own = moved(first, lambda i, j, k: (i, j, k))
    partial = pl.pallas_call(
        begin,
        out_shape=jax.ShapeDtypeStruct(amplitudes.shape, jnp.float32),
        in_specs=[vmem, vmem, smem, vmem],
        out_specs=vmem,
        scratch_shapes=[pltpu.VMEM((w * w, w), jnp.float32)],
        compiler_params=params,
        name="begin",
    )(swap_bc, amplitudes, energy_a, shift_bc)
    return pl.pallas_call(
        finish,
        out_shape=jax.ShapeDtypeStruct(amplitudes.shape, jnp.bfloat16),
        in_specs=[vmem, vmem, vmem],
        out_specs=vmem,
        scratch_shapes=[pltpu.VMEM((w * w, w), jnp.float32)],
        compiler_params=params,
        name="finish",
    )(own, swap_ab, partial)


def solution(mesh):
    fine = Mesh(mesh.devices.reshape(2, 4, 8, 4, 2), ALL)
    place = P(("zh", "y"), "zl", ("x", "core"))
    return jax.shard_map(on_device, mesh=fine, in_specs=(place, P(), P()), out_specs=place, check_vma=False)
```

```python
import functools

import jax
import jax.numpy as jnp
import numpy as np
from jax import lax
from jax.experimental import pallas as pl
from jax.experimental.pallas import tpu as pltpu
from jax.sharding import Mesh, PartitionSpec as P

ALL = ("zh", "y", "zl", "x", "core")
PLANE = ("y", "x", "core")
UPPER = [(u, v) for u in range(4) for v in range(u + 1, 4)]
LAST = (((1,), (1,)), ((), ()))
PLACES = (
    (0, 26, 8, 4, 5, 1, 12, 30, 9, 10, 20, 2, 24, 22, 14, 6, 21, 15, 18, 28, 11, 16, 31, 23, 3, 27, 13, 17, 7, 29, 19, 25),
    (4, 30, 2, 6, 0, 10, 31, 1, 12, 14, 15, 8, 11, 13, 16, 20, 18, 22, 28, 9, 29, 21, 24, 3, 25, 26, 19, 27, 17, 23, 5, 7),
    (2, 24, 28, 0, 30, 6, 10, 12, 8, 31, 11, 20, 13, 4, 3, 14, 22, 16, 17, 18, 23, 19, 21, 25, 7, 1, 29, 15, 26, 27, 5, 9),
    (6, 28, 30, 0, 12, 10, 2, 22, 20, 8, 14, 7, 11, 18, 4, 16, 26, 15, 21, 9, 13, 23, 24, 3, 5, 17, 1, 27, 31, 19, 25, 29),
    (8, 2, 26, 3, 30, 4, 12, 0, 20, 14, 5, 9, 15, 6, 18, 16, 22, 24, 10, 25, 19, 13, 7, 21, 28, 11, 23, 17, 29, 1, 31, 27),
    (16, 0, 4, 22, 18, 12, 24, 26, 10, 14, 15, 8, 2, 9, 11, 20, 28, 3, 1, 27, 19, 30, 23, 13, 17, 5, 6, 29, 31, 7, 25, 21),
    (30, 12, 2, 24, 28, 14, 0, 4, 10, 16, 8, 29, 13, 6, 15, 26, 25, 11, 22, 20, 17, 21, 18, 23, 1, 27, 19, 3, 31, 7, 9, 5),
    (8, 14, 20, 2, 24, 6, 4, 26, 16, 10, 18, 30, 5, 0, 12, 11, 17, 21, 15, 22, 9, 1, 13, 28, 3, 23, 29, 7, 25, 19, 31, 27),
    (30, 12, 6, 2, 26, 4, 0, 18, 20, 3, 7, 8, 10, 1, 24, 13, 31, 25, 16, 27, 5, 22, 14, 21, 15, 28, 19, 17, 23, 9, 29, 11),
    (12, 22, 28, 24, 30, 4, 8, 6, 2, 14, 10, 11, 13, 18, 7, 16, 19, 0, 20, 9, 15, 29, 25, 26, 23, 17, 21, 27, 3, 31, 5, 1),
    (4, 12, 2, 6, 28, 18, 14, 8, 0, 3, 26, 5, 15, 7, 10, 19, 16, 22, 24, 20, 21, 27, 23, 25, 17, 30, 11, 13, 31, 29, 1, 9),
    (24, 14, 28, 2, 8, 9, 20, 4, 15, 12, 0, 10, 21, 16, 13, 6, 22, 26, 3, 7, 11, 17, 18, 25, 5, 27, 1, 30, 23, 19, 29, 31),
    (4, 0, 1, 12, 6, 5, 30, 2, 24, 26, 25, 22, 8, 14, 10, 20, 21, 18, 9, 16, 11, 28, 19, 15, 27, 17, 7, 29, 13, 3, 31, 23),
    (4, 24, 18, 6, 2, 12, 0, 5, 13, 14, 10, 8, 3, 15, 9, 16, 17, 20, 22, 26, 11, 30, 1, 28, 21, 31, 25, 19, 27, 23, 29, 7),
    (6, 26, 4, 28, 12, 7, 14, 0, 13, 8, 18, 9, 22, 10, 15, 2, 27, 29, 19, 16, 20, 24, 23, 21, 17, 30, 31, 1, 25, 3, 11, 5),
    (30, 10, 31, 8, 16, 20, 2, 4, 14, 6, 28, 3, 9, 12, 11, 15, 22, 17, 7, 18, 0, 13, 1, 26, 27, 29, 19, 21, 5, 24, 23, 25),
)


def holder(i, j, k):
    place = PLACES[(i >> 2) * 8 + j][(i & 3) * 8 + k]
    return (((i >> 2) * 4 + place // 8) * 8 + j) * 8 + place % 8


def moved(array, target):
    pairs = []
    for i in range(8):
        for j in range(8):
            for k in range(8):
                a, b, c = target(i, j, k)
                pairs.append((holder(i, j, k), (a * 8 + b) * 8 + c))
    return lax.ppermute(array, ALL, pairs)


def pack(amps_ref, out_ref, rows):
    w = amps_ref.shape[0]
    rows[...] = amps_ref[...].astype(jnp.float32).reshape(w * w, w)
    for d in range(w // 2):
        pair = [rows[pl.ds(2 * d + b, w, stride=w), :] for b in range(2)]
        out_ref[d] = jnp.concatenate(pair, axis=1).astype(jnp.bfloat16)
    for d in range(w // 2, 32):
        out_ref[d] = jnp.zeros((w, 2 * w), jnp.bfloat16)


def near_part(half_ref, rows_ref, factors_ref, total_ref, other_ref, matrix):
    w = rows_ref.shape[1]
    half = half_ref[0]
    first = half == 0
    own = pl.ds(pl.multiple_of(half * 4 * w, 64), 4 * w)
    other = pl.ds(pl.multiple_of((1 - half) * 4 * w, 64), 4 * w)
    mine = jnp.concatenate([factors_ref[p, own, :] for p in range(4)], axis=0)
    for p in range(4):
        other_ref[p] = jnp.where(first, factors_ref[p, :, 4 * w :], factors_ref[p, :, : 4 * w])
    zero = jnp.zeros((4 * w, 4 * w), jnp.bfloat16)
    for b in range(2):
        part = slice(b * w, (b + 1) * w)
        near = jnp.concatenate(
            [jnp.concatenate([rows_ref[y * 8 + k, :, part] for k in range(8)], axis=1) for y in range(4)], axis=0
        )
        across = jnp.where(first, near[:, 4 * w :], near[:, : 4 * w])
        below = -across.astype(jnp.float32).T.astype(jnp.bfloat16)
        matrix[own, :] = near
        matrix[other, :] = jnp.where(
            first, jnp.concatenate([below, zero], axis=1), jnp.concatenate([zero, below], axis=1)
        )
        along = jnp.dot(mine, matrix[...], preferred_element_type=jnp.float32).astype(jnp.bfloat16)
        total = jnp.zeros((4 * w, 8 * w), jnp.float32)
        for p in range(4):
            total += lax.dot_general(
                along[p * 4 * w : (p + 1) * 4 * w], factors_ref[p], LAST, preferred_element_type=jnp.float32
            )
        total_ref[b] = total


def far_part(half_ref, slot_ref, total_ref, far_ref, other_ref, out_ref):
    w = far_ref.shape[0]
    own = pl.ds(pl.multiple_of(half_ref[0] * 4 * w, 64), 4 * w)
    mine = jnp.concatenate([other_ref[p, own, :] for p in range(4)], axis=0)
    zero = jnp.zeros((w, w), jnp.float32)
    row = lax.broadcasted_iota(jnp.int32, (w, w), 0)
    column = lax.broadcasted_iota(jnp.int32, (w, w), 1)
    results = []
    for b in range(2):
        blocks = [far_ref[:, (2 * n + b) * w : (2 * n + b + 1) * w].astype(jnp.float32) for n in range(8)]
        found = dict(zip(UPPER, blocks))
        for n in range(2):
            found[2 * n, 2 * n] = jnp.where(row < column, blocks[6 + n], zero)
            found[2 * n + 1, 2 * n + 1] = jnp.where(row > column, blocks[6 + n], zero)
        part = [jnp.concatenate([found.get((u, v), zero) for v in range(4)], axis=1) for u in range(4)]
        part = jnp.concatenate(part, axis=0).astype(jnp.bfloat16)
        along = jnp.dot(mine, part, preferred_element_type=jnp.float32)
        along -= lax.dot_general(mine, part, LAST, preferred_element_type=jnp.float32)
        along = along.astype(jnp.bfloat16)
        total = total_ref[b]
        for p in range(4):
            total += lax.dot_general(
                along[p * 4 * w : (p + 1) * 4 * w], other_ref[p], LAST, preferred_element_type=jnp.float32
            )
        results.append(total)
    for y in range(4):
        for k in range(8):
            tile = [r[y * w : (y + 1) * w, k * w : (k + 1) * w] for r in results]
            out_ref[slot_ref[y * 8 + k]] = jnp.concatenate(tile, axis=1).astype(jnp.bfloat16)


def begin(ab_ref, amps_ref, shift_a_ref, shift_bc_ref, sum_ref):
    w = amps_ref.shape[0]
    shift_bc = shift_bc_ref[...]
    for a in range(w):
        shift = shift_bc + shift_a_ref[a]
        swapped = ab_ref[:, a * w : (a + 1) * w].astype(jnp.float32)
        sum_ref[a] = shift * amps_ref[a].astype(jnp.float32) - 2.0 * swapped


def finish(own_ref, bc_ref, sum_ref, out_ref, own_rows, bc_rows):
    w = bc_ref.shape[0]
    for n in range(w):
        part = slice(n * w, (n + 1) * w)
        own_rows[pl.ds(n, w, stride=w), :] = own_ref[:, part].astype(jnp.float32)
        bc_rows[pl.ds(n, w, stride=w), :] = bc_ref[:, part].astype(jnp.float32)
    turned = bc_rows[...].T
    for a in range(w):
        part = slice(a * w, (a + 1) * w)
        ladder = own_rows[part, :] - turned[:, part]
        out_ref[a] = (sum_ref[a] + 2.0 * ladder).astype(jnp.bfloat16)


def on_device(amplitudes, factors, energies):
    w = amplitudes.shape[0]
    half = lax.axis_index("zh")
    index_a = half * 4 + lax.axis_index("y")
    index_b = lax.axis_index("zl")
    index_c = lax.axis_index("x") * 2 + lax.axis_index("core")
    energy_a = lax.dynamic_slice_in_dim(energies, index_a * w, w, 0)
    energy_b = lax.dynamic_slice_in_dim(energies, index_b * w, w, 0)
    energy_c = lax.dynamic_slice_in_dim(energies, index_c * w, w, 0)
    shift_bc = energy_b[:, None] + energy_c[None, :]
    places = jnp.asarray(np.array(PLACES), jnp.int32)[half * 8 + index_b]

    smem = pl.BlockSpec(memory_space=pltpu.SMEM)
    vmem = pl.BlockSpec(memory_space=pltpu.VMEM)
    params = pltpu.CompilerParams(vmem_limit_bytes=40 << 20)
    parts = pl.pallas_call(
        pack,
        out_shape=jax.ShapeDtypeStruct((32, w, 2 * w), jnp.bfloat16),
        in_specs=[vmem],
        out_specs=vmem,
        scratch_shapes=[pltpu.VMEM((w * w, w), jnp.float32)],
        compiler_params=params,
        name="pack",
    )(amplitudes)
    parts = lax.all_to_all(parts, PLANE, split_axis=0, concat_axis=0, tiled=True)
    near = lax.dynamic_slice_in_dim(parts.reshape(4, 8, w, 2 * w), half * 4, 4, 1)
    above = np.arange(w)[:, None] < np.arange(2 * w)[None, :] % w
    mixed = [jnp.where(above, near[2 * n, 2 * n], near[2 * n + 1, 2 * n + 1]) for n in range(2)]
    near = jnp.concatenate([near[u, v] for u, v in UPPER] + mixed, axis=1)
    far = lax.ppermute(near, "zh", [(0, 1), (1, 0)])
    total, other = pl.pallas_call(
        near_part,
        out_shape=(
            jax.ShapeDtypeStruct((2, 4 * w, 8 * w), jnp.float32),
            jax.ShapeDtypeStruct((4, 8 * w, 4 * w), jnp.bfloat16),
        ),
        in_specs=[smem, vmem, vmem],
        out_specs=(vmem, vmem),
        scratch_shapes=[pltpu.VMEM((8 * w, 8 * w), jnp.bfloat16)],
        compiler_params=params,
        name="near_part",
    )(half.reshape(1), parts, factors)
    close = pl.pallas_call(
        far_part,
        out_shape=jax.ShapeDtypeStruct((32, w, 2 * w), jnp.bfloat16),
        in_specs=[smem, smem, vmem, vmem, vmem],
        out_specs=vmem,
        compiler_params=params,
        name="far_part",
    )(half.reshape(1), places, total, far, other)
    close = lax.all_to_all(close, PLANE, split_axis=0, concat_axis=0, tiled=True)[:24]
    first = close.transpose(1, 0, 2).reshape(w, w * w)
    swap_ab = moved(first, lambda i, j, k: (j, i, k))
    swap_bc = moved(first, lambda i, j, k: (i, k, j))
    own = moved(first, lambda i, j, k: (i, j, k))
    partial = pl.pallas_call(
        begin,
        out_shape=jax.ShapeDtypeStruct(amplitudes.shape, jnp.float32),
        in_specs=[vmem, vmem, smem, vmem],
        out_specs=vmem,
        compiler_params=params,
        name="begin",
    )(swap_ab, amplitudes, energy_a, shift_bc)
    return pl.pallas_call(
        finish,
        out_shape=jax.ShapeDtypeStruct(amplitudes.shape, jnp.bfloat16),
        in_specs=[vmem, vmem, vmem],
        out_specs=vmem,
        scratch_shapes=[pltpu.VMEM((w * w, w), jnp.float32)] * 2,
        compiler_params=params,
        name="finish",
    )(own, swap_bc, partial)


def solution(mesh):
    fine = Mesh(mesh.devices.reshape(2, 4, 8, 4, 2), ALL)
    place = P(("zh", "y"), "zl", ("x", "core"))
    return jax.shard_map(on_device, mesh=fine, in_specs=(place, P(), P()), out_specs=place, check_vma=False)
```

```python
import functools

import jax
import jax.numpy as jnp
import numpy as np
from jax import lax
from jax.experimental import pallas as pl
from jax.experimental.pallas import tpu as pltpu
from jax.sharding import Mesh, PartitionSpec as P

ALL = ("zh", "y", "zl", "x", "core")
PLANE = ("y", "x", "core")
UPPER = [(u, v) for u in range(4) for v in range(u + 1, 4)]
LAST = (((1,), (1,)), ((), ()))
PLACES = (
    (12, 26, 2, 8, 30, 3, 6, 0, 1, 10, 9, 22, 16, 14, 13, 20, 24, 23, 31, 27, 4, 18, 21, 17, 11, 7, 5, 28, 15, 19, 25, 29),
    (14, 6, 26, 16, 24, 4, 30, 5, 12, 8, 20, 10, 22, 9, 11, 13, 27, 0, 2, 15, 21, 7, 18, 23, 1, 25, 28, 17, 19, 31, 3, 29),
    (0, 4, 12, 26, 10, 8, 2, 14, 5, 20, 30, 13, 6, 27, 3, 9, 15, 24, 22, 18, 16, 19, 17, 23, 31, 28, 1, 29, 21, 7, 11, 25),
    (2, 4, 10, 26, 16, 12, 3, 28, 14, 6, 18, 13, 0, 11, 15, 8, 9, 20, 17, 7, 22, 21, 23, 29, 1, 30, 19, 27, 31, 24, 5, 25),
    (6, 12, 2, 26, 7, 3, 0, 8, 10, 20, 13, 16, 9, 21, 22, 14, 30, 11, 28, 18, 15, 4, 17, 24, 25, 1, 23, 29, 27, 5, 19, 31),
    (24, 22, 0, 20, 4, 16, 5, 26, 12, 8, 14, 13, 10, 15, 9, 11, 28, 1, 2, 21, 23, 6, 27, 18, 25, 7, 29, 3, 17, 19, 30, 31),
    (28, 14, 6, 8, 4, 5, 24, 26, 16, 30, 10, 2, 0, 12, 20, 3, 15, 25, 18, 9, 22, 21, 23, 11, 7, 13, 19, 31, 1, 17, 29, 27),
    (0, 10, 12, 6, 2, 18, 4, 7, 11, 1, 26, 13, 14, 22, 3, 8, 19, 23, 15, 16, 17, 20, 21, 9, 28, 27, 24, 29, 30, 31, 5, 25),
    (30, 2, 0, 4, 6, 3, 1, 26, 22, 8, 20, 9, 10, 14, 16, 12, 7, 24, 28, 17, 13, 29, 18, 23, 25, 11, 19, 27, 31, 21, 15, 5),
    (4, 6, 26, 12, 14, 28, 22, 24, 10, 8, 20, 16, 11, 9, 13, 15, 23, 29, 17, 2, 0, 18, 7, 21, 30, 5, 27, 3, 25, 19, 1, 31),
    (4, 2, 5, 18, 6, 28, 0, 26, 16, 14, 8, 12, 13, 10, 3, 7, 17, 22, 24, 19, 20, 15, 9, 23, 30, 29, 1, 31, 11, 21, 25, 27),
    (6, 2, 0, 10, 26, 8, 20, 4, 12, 11, 18, 9, 22, 13, 14, 24, 5, 15, 30, 3, 7, 16, 17, 27, 1, 23, 28, 21, 29, 25, 19, 31),
    (4, 0, 8, 5, 26, 30, 2, 6, 14, 22, 9, 1, 10, 20, 11, 7, 3, 12, 16, 23, 18, 31, 28, 21, 13, 15, 24, 27, 25, 17, 19, 29),
    (30, 2, 4, 5, 0, 16, 6, 22, 14, 8, 3, 12, 10, 15, 11, 13, 7, 18, 28, 20, 17, 19, 24, 23, 9, 26, 27, 29, 25, 1, 21, 31),
    (6, 26, 30, 18, 2, 4, 7, 14, 28, 5, 8, 3, 9, 12, 31, 10, 13, 19, 16, 20, 15, 22, 21, 24, 11, 0, 23, 25, 29, 17, 1, 27),
    (28, 8, 2, 0, 14, 29, 6, 7, 10, 9, 22, 3, 4, 26, 15, 12, 24, 25, 11, 16, 17, 13, 18, 20, 27, 5, 21, 23, 19, 1, 30, 31),
)


def holder(i, j, k):
    place = PLACES[(i >> 2) * 8 + j][(i & 3) * 8 + k]
    return (((i >> 2) * 4 + place // 8) * 8 + j) * 8 + place % 8


def moved(array, target):
    pairs = []
    for i in range(8):
        for j in range(8):
            for k in range(8):
                a, b, c = target(i, j, k)
                pairs.append((holder(i, j, k), (a * 8 + b) * 8 + c))
    return lax.ppermute(array, ALL, pairs)


def pack(amps_ref, out_ref, rows):
    w = amps_ref.shape[0]
    rows[...] = amps_ref[...].astype(jnp.float32).reshape(w * w, w)
    for d in range(w // 2):
        pair = [rows[pl.ds(2 * d + b, w, stride=w), :] for b in range(2)]
        out_ref[d] = jnp.concatenate(pair, axis=1).astype(jnp.bfloat16)
    for d in range(w // 2, 32):
        out_ref[d] = jnp.zeros((w, 2 * w), jnp.bfloat16)


def near_part(half_ref, rows_ref, factors_ref, total_ref, other_ref, matrix):
    w = rows_ref.shape[1]
    half = half_ref[0]
    first = half == 0
    own = pl.ds(pl.multiple_of(half * 4 * w, 64), 4 * w)
    other = pl.ds(pl.multiple_of((1 - half) * 4 * w, 64), 4 * w)
    mine = jnp.concatenate([factors_ref[p, own, :] for p in range(4)], axis=0)
    for p in range(4):
        other_ref[p] = jnp.where(first, factors_ref[p, :, 4 * w :], factors_ref[p, :, : 4 * w])
    zero = jnp.zeros((4 * w, 4 * w), jnp.bfloat16)
    for b in range(2):
        part = slice(b * w, (b + 1) * w)
        near = jnp.concatenate(
            [jnp.concatenate([rows_ref[y * 8 + k, :, part] for k in range(8)], axis=1) for y in range(4)], axis=0
        )
        across = jnp.where(first, near[:, 4 * w :], near[:, : 4 * w])
        below = -across.astype(jnp.float32).T.astype(jnp.bfloat16)
        matrix[own, :] = near
        matrix[other, :] = jnp.where(
            first, jnp.concatenate([below, zero], axis=1), jnp.concatenate([zero, below], axis=1)
        )
        along = jnp.dot(mine, matrix[...], preferred_element_type=jnp.float32).astype(jnp.bfloat16)
        total = jnp.zeros((4 * w, 8 * w), jnp.float32)
        for p in range(4):
            total += lax.dot_general(
                along[p * 4 * w : (p + 1) * 4 * w], factors_ref[p], LAST, preferred_element_type=jnp.float32
            )
        total_ref[b] = total


def far_part(half_ref, slot_ref, total_ref, far_ref, other_ref, out_ref):
    w = far_ref.shape[0]
    own = pl.ds(pl.multiple_of(half_ref[0] * 4 * w, 64), 4 * w)
    mine = jnp.concatenate([other_ref[p, own, :] for p in range(4)], axis=0)
    zero = jnp.zeros((w, w), jnp.float32)
    row = lax.broadcasted_iota(jnp.int32, (w, w), 0)
    column = lax.broadcasted_iota(jnp.int32, (w, w), 1)
    results = []
    for b in range(2):
        blocks = [far_ref[:, (2 * n + b) * w : (2 * n + b + 1) * w].astype(jnp.float32) for n in range(8)]
        found = dict(zip(UPPER, blocks))
        for n in range(2):
            found[2 * n, 2 * n] = jnp.where(row < column, blocks[6 + n], zero)
            found[2 * n + 1, 2 * n + 1] = jnp.where(row > column, blocks[6 + n], zero)
        part = [jnp.concatenate([found.get((u, v), zero) for v in range(4)], axis=1) for u in range(4)]
        part = jnp.concatenate(part, axis=0).astype(jnp.bfloat16)
        along = jnp.dot(mine, part, preferred_element_type=jnp.float32)
        along -= lax.dot_general(mine, part, LAST, preferred_element_type=jnp.float32)
        along = along.astype(jnp.bfloat16)
        total = total_ref[b]
        for p in range(4):
            total += lax.dot_general(
                along[p * 4 * w : (p + 1) * 4 * w], other_ref[p], LAST, preferred_element_type=jnp.float32
            )
        results.append(total)
    for y in range(4):
        for k in range(8):
            tile = [r[y * w : (y + 1) * w, k * w : (k + 1) * w] for r in results]
            out_ref[slot_ref[y * 8 + k]] = jnp.concatenate(tile, axis=1).astype(jnp.bfloat16)


def begin(bc_ref, amps_ref, shift_a_ref, shift_bc_ref, sum_ref, rows):
    w = amps_ref.shape[0]
    shift_bc = shift_bc_ref[...]
    for n in range(w):
        rows[pl.ds(n, w, stride=w), :] = bc_ref[:, n * w : (n + 1) * w].astype(jnp.float32)
    turned = rows[...].T
    for a in range(w):
        shift = shift_bc + shift_a_ref[a]
        sum_ref[a] = shift * amps_ref[a].astype(jnp.float32) - 2.0 * turned[:, a * w : (a + 1) * w]


def finish(own_ref, ab_ref, sum_ref, out_ref, rows):
    w = ab_ref.shape[0]
    for n in range(w):
        rows[pl.ds(n, w, stride=w), :] = own_ref[:, n * w : (n + 1) * w].astype(jnp.float32)
    for a in range(w):
        part = slice(a * w, (a + 1) * w)
        ladder = rows[part, :] - ab_ref[:, part].astype(jnp.float32)
        out_ref[a] = (sum_ref[a] + 2.0 * ladder).astype(jnp.bfloat16)


def on_device(amplitudes, factors, energies):
    w = amplitudes.shape[0]
    half = lax.axis_index("zh")
    index_a = half * 4 + lax.axis_index("y")
    index_b = lax.axis_index("zl")
    index_c = lax.axis_index("x") * 2 + lax.axis_index("core")
    energy_a = lax.dynamic_slice_in_dim(energies, index_a * w, w, 0)
    energy_b = lax.dynamic_slice_in_dim(energies, index_b * w, w, 0)
    energy_c = lax.dynamic_slice_in_dim(energies, index_c * w, w, 0)
    shift_bc = energy_b[:, None] + energy_c[None, :]
    places = jnp.asarray(np.array(PLACES), jnp.int32)[half * 8 + index_b]

    smem = pl.BlockSpec(memory_space=pltpu.SMEM)
    vmem = pl.BlockSpec(memory_space=pltpu.VMEM)
    params = pltpu.CompilerParams(vmem_limit_bytes=40 << 20)
    parts = pl.pallas_call(
        pack,
        out_shape=jax.ShapeDtypeStruct((32, w, 2 * w), jnp.bfloat16),
        in_specs=[vmem],
        out_specs=vmem,
        scratch_shapes=[pltpu.VMEM((w * w, w), jnp.float32)],
        compiler_params=params,
        name="pack",
    )(amplitudes)
    parts = lax.all_to_all(parts, PLANE, split_axis=0, concat_axis=0, tiled=True)
    near = lax.dynamic_slice_in_dim(parts.reshape(4, 8, w, 2 * w), half * 4, 4, 1)
    above = np.arange(w)[:, None] < np.arange(2 * w)[None, :] % w
    mixed = [jnp.where(above, near[2 * n, 2 * n], near[2 * n + 1, 2 * n + 1]) for n in range(2)]
    near = jnp.concatenate([near[u, v] for u, v in UPPER] + mixed, axis=1)
    far = lax.ppermute(near, "zh", [(0, 1), (1, 0)])
    total, other = pl.pallas_call(
        near_part,
        out_shape=(
            jax.ShapeDtypeStruct((2, 4 * w, 8 * w), jnp.float32),
            jax.ShapeDtypeStruct((4, 8 * w, 4 * w), jnp.bfloat16),
        ),
        in_specs=[smem, vmem, vmem],
        out_specs=(vmem, vmem),
        scratch_shapes=[pltpu.VMEM((8 * w, 8 * w), jnp.bfloat16)],
        compiler_params=params,
        name="near_part",
    )(half.reshape(1), parts, factors)
    close = pl.pallas_call(
        far_part,
        out_shape=jax.ShapeDtypeStruct((32, w, 2 * w), jnp.bfloat16),
        in_specs=[smem, smem, vmem, vmem, vmem],
        out_specs=vmem,
        compiler_params=params,
        name="far_part",
    )(half.reshape(1), places, total, far, other)
    close = lax.all_to_all(close, PLANE, split_axis=0, concat_axis=0, tiled=True)[:24]
    first = close.transpose(1, 0, 2).reshape(w, w * w)
    swap_ab = moved(first, lambda i, j, k: (j, i, k))
    swap_bc = moved(first, lambda i, j, k: (i, k, j))
    own = moved(first, lambda i, j, k: (i, j, k))
    partial = pl.pallas_call(
        begin,
        out_shape=jax.ShapeDtypeStruct(amplitudes.shape, jnp.float32),
        in_specs=[vmem, vmem, smem, vmem],
        out_specs=vmem,
        scratch_shapes=[pltpu.VMEM((w * w, w), jnp.float32)],
        compiler_params=params,
        name="begin",
    )(swap_bc, amplitudes, energy_a, shift_bc)
    return pl.pallas_call(
        finish,
        out_shape=jax.ShapeDtypeStruct(amplitudes.shape, jnp.bfloat16),
        in_specs=[vmem, vmem, vmem],
        out_specs=vmem,
        scratch_shapes=[pltpu.VMEM((w * w, w), jnp.float32)],
        compiler_params=params,
        name="finish",
    )(own, swap_ab, partial)


def solution(mesh):
    fine = Mesh(mesh.devices.reshape(2, 4, 8, 4, 2), ALL)
    place = P(("zh", "y"), "zl", ("x", "core"))
    return jax.shard_map(on_device, mesh=fine, in_specs=(place, P(), P()), out_specs=place, check_vma=False)
```
